128 devices in a mesh: outer: 4 (over y), blk: 16 (over x_hi, z, core), tp: 2 (over x_lo).
Axes of the slice: x: 4 (x_hi: 2, x_lo: 2; x = x_hi * 2 + x_lo), y: 4, z: 4, core: 2. Of those that a mesh axis runs over, the one named last changes fastest.
Arguments:
- img_embed: bfloat16 [4, 4096, 1152], P('outer', 'blk'), may hold values from -0.4375 to 0.4375
- txt_embed: bfloat16 [4, 4096, 1152], P('outer', 'blk'), may hold values from -0.4375 to 0.4375
- img_hidden: bfloat16 [4, 4096, 4304], P('outer', 'blk', 'tp'), may hold values from -1.5 to 1.5
- txt_hidden: bfloat16 [4, 4096, 4304], P('outer', 'blk', 'tp'), may hold values from -1.5 to 1.5
- proj_weights: bfloat16 [2, 4304, 1152], P(None, 'tp'), may hold values from -0.09375 to 0.09375
- residual_in: float32 [4, 1152, 2, 4304], P('outer', 'blk', None, 'tp'), may hold values from -6 to 6
- partner: int32 [4, 4096], P('outer', ('blk', 'tp')), may hold values from 0 to 4095, each once within a row
- group_ids: int32 [2, 4304], P(None, 'tp'), may hold values from 0 to 7, as said below
- logit_scale: float32 [1], replicated, may hold values from 4 to 12
- logit_bias: float32 [1], replicated, may hold values from -4 to -1
- loss_scale: float32 [1], replicated, may hold values from 256 to 1024
Outputs:
- d_img_hidden: bfloat16 [4, 4096, 4304], P('outer', 'blk', 'tp')
- d_txt_hidden: bfloat16 [4, 4096, 4304], P('outer', 'blk', 'tp')
- summed: float32 [1152, 2, 4304], P('blk', None, 'tp')
- residual_out: float32 [4, 1152, 2, 4304], P('outer', 'blk', None, 'tp')
The draws below stay inside these ranges and needn't reach their ends.
Inputs may be any that keep to these rules, and one draw needn't show every extreme that they name: `group_ids`: within each tower, every group id appears among the first 8 units of each of the 2 consecutive slices of 4304 / 2 units. `partner`: each pod's row is a permutation of its 4096 text indices.
All inputs are finite; a program needn't handle non-finite values.
Results may differ from the reference program's by a relative error of at most 0.034.
Values may be sent and summed in bfloat16 or wider, within the bound.
No kernel may reach another device: no remote copies, remote signals or barrier semaphores. Data moves between devices by JAX's collectives and lax.ppermute only.
A program may use at most 128 MiB of HBM per device.

```python
import math
import jax
import jax.numpy as jnp
from jax import lax

E = 1152
FF = 4304
ROWS = 256
NG = 8
POD = 4096
N_OUTER = 4
N_BLK = 16
N_TP = 2


def draw_group_ids(key, part):
    key = jax.random.fold_in(key, 7)
    ids = jax.random.randint(key, (2, FF), 0, NG, dtype=jnp.int32)
    local = FF // N_TP
    lead = (jnp.arange(N_TP, dtype=jnp.int32)[:, None] * local + jnp.arange(NG, dtype=jnp.int32)[None, :]).reshape(-1)
    values = jnp.tile(jnp.arange(NG, dtype=jnp.int32), N_TP)
    return ids.at[:, lead].set(values[None, :])


def block_levels(stream_key, extent, split, least, largest):
    loudness, own = 1.0, jax.random.fold_in(stream_key, 6)
    for dim, parts in split:
        heights = jnp.exp(jax.random.uniform(jax.random.fold_in(own, dim), (parts,), jnp.float32, least / len(split), largest / len(split)))
        loudness = loudness * jnp.repeat(heights, extent[dim] // parts).reshape([-1 if axis == dim else 1 for axis in range(len(extent))])
    return loudness


def centred(stream_key, extent, width, reach, split=(), kind=jnp.bfloat16):
    entries = width * jax.random.normal(stream_key, extent, jnp.float32)
    if split:
        entries = entries * block_levels(stream_key, extent, split, -0.22, 0.18)
    return jnp.clip(entries, -reach, reach).astype(kind)


def setup_inputs(seed: int = 0) -> dict:
    seeds = jax.random.split(jax.random.key(seed), 12)
    return {
        "img_embed": centred(seeds[0], (N_OUTER, POD, E), 0.03, 0.4375, ((0, 4), (1, 16))),
        "txt_embed": centred(seeds[1], (N_OUTER, POD, E), 0.03, 0.4375, ((0, 4), (1, 16))),
        "img_hidden": centred(seeds[2], (N_OUTER, POD, FF), 0.1, 1.5, ((0, 4), (1, 16), (2, 2))),
        "txt_hidden": centred(seeds[3], (N_OUTER, POD, FF), 0.1, 1.5, ((0, 4), (1, 16), (2, 2))),
        "proj_weights": centred(seeds[4], (2, FF, E), FF ** -0.5, 0.09375, ((1, 2),)),
        "residual_in": centred(seeds[5], (N_OUTER, E, 2, FF), 1.0, 6.0, ((0, 4), (1, 16), (3, 2)), jnp.float32),
        "partner": jax.vmap(lambda own: jax.random.permutation(own, POD))(jax.random.split(seeds[6], N_OUTER)).reshape((N_OUTER, POD)).astype(jnp.int32),
        "group_ids": draw_group_ids(jax.random.fold_in(seeds[11], 71), 0),
        "logit_scale": jnp.clip(jax.random.uniform(seeds[8], (1,), jnp.float32, 4.0, 12.0), 4.0, 12.0),
        "logit_bias": jnp.clip(jax.random.uniform(seeds[9], (1,), jnp.float32, -4.0, -1.0), -4.0, -1.0),
        "loss_scale": jnp.clip(jnp.exp(jax.random.uniform(seeds[10], (1,), jnp.float32, math.log(256.0), math.log(1024.0))), 256.0, 1024.0),
    }


EPS = 1e-06

def normed(embed):
    e32 = embed.astype(jnp.float32)
    inverse = lax.rsqrt(lax.optimization_barrier(jnp.sum(e32 * e32, axis=-1, keepdims=True)) + 1e-06)
    return (e32 * inverse, inverse)

def embed_grad(z32, inverse, dz):
    return ((dz - z32 * lax.optimization_barrier(jnp.sum(z32 * dz, axis=-1, keepdims=True))) * inverse).astype(jnp.bfloat16)

def reference(img_embed, txt_embed, img_hidden, txt_hidden, proj_weights, residual_in, partner, group_ids, logit_scale, logit_bias, loss_scale):
    scale = logit_scale[0]
    bias = logit_bias[0]
    factor = loss_scale[0] / POD
    local = FF // N_TP
    ids = group_ids.reshape(2, N_TP, local)
    onehot = (ids[:, :, :, None] == jnp.arange(NG, dtype=jnp.int32)[None, None, None, :]).astype(jnp.float32)
    count = lax.optimization_barrier(jnp.sum(onehot, axis=2)) * (E // N_BLK)
    w_img = proj_weights[0].astype(jnp.float32)
    w_txt = proj_weights[1].astype(jnp.float32)
    d_img_list, d_txt_list, res_list = ([], [], [])
    total = jnp.zeros((E, 2, FF), jnp.float32)
    for pod in range(N_OUTER):
        zi32, inv_i = normed(img_embed[pod])
        zt32, inv_t = normed(txt_embed[pod])
        zi = zi32.astype(jnp.bfloat16).astype(jnp.float32)
        zt = zt32.astype(jnp.bfloat16).astype(jnp.float32)
        logits = scale * jnp.dot(zi, zt.T) + bias
        positive = (partner[pod][:, None] == jnp.arange(POD, dtype=jnp.int32)[None, :]).astype(jnp.float32)
        weights = ((jax.nn.sigmoid(logits) - positive) * factor).astype(jnp.bfloat16).astype(jnp.float32)
        dzi = scale * jnp.dot(weights, zt)
        dzt = scale * jnp.dot(weights.T, zi)
        de_img = embed_grad(zi32, inv_i, dzi)
        de_txt = embed_grad(zt32, inv_t, dzt)
        d_img_list.append(jnp.dot(de_img.astype(jnp.float32), w_img.T).astype(jnp.bfloat16))
        d_txt_list.append(jnp.dot(de_txt.astype(jnp.float32), w_txt.T).astype(jnp.bfloat16))
        stacked = jnp.stack([de_img, de_txt]).astype(jnp.float32).reshape(2, N_BLK, ROWS, E).transpose(1, 0, 2, 3)
        hidden = jnp.stack([img_hidden[pod], txt_hidden[pod]]).astype(jnp.float32).reshape(2, N_BLK, ROWS, FF).transpose(1, 0, 2, 3)

        def add_block(carry, pieces):
            part = jnp.einsum('kre,krf->ekf', pieces[0], pieces[1])
            rounded = lax.optimization_barrier(part.astype(jnp.bfloat16))
            return (carry + rounded.astype(jnp.float32), None)
        grad, _ = lax.scan(add_block, jnp.zeros((E, 2, FF), jnp.float32), (stacked, hidden))
        g = grad + residual_in[pod]
        tiles = g.reshape(N_BLK, E // N_BLK, 2, N_TP, local)
        absum = lax.optimization_barrier(jnp.sum(jnp.abs(tiles), axis=1))
        group_total = jnp.einsum('bktf,ktfg->bktg', absum, onehot, precision=lax.Precision.HIGHEST)
        level = group_total / count[None] + EPS
        spread = jnp.einsum('bktg,ktfg->bktf', level, onehot, precision=lax.Precision.HIGHEST)[:, None]
        packed = spread * jnp.tanh(tiles / spread)
        res_list.append((tiles - packed).reshape(E, 2, FF))
        total = total + packed.reshape(E, 2, FF)
    return (jnp.stack(d_img_list), jnp.stack(d_txt_list), total, jnp.stack(res_list))
```

```python
import jax
import jax.numpy as jnp
from jax import lax
from jax.sharding import PartitionSpec as P

NG = 8
EPS = 1e-06
AXES = ("outer", "blk", "tp")
F32 = jnp.float32
BF16 = jnp.bfloat16


def moved(where):
    pairs = []
    for y in range(4):
        for x in range(4):
            for z in range(4):
                for c in range(2):
                    x2, y2, z2, c2 = where(x, y, z, c)
                    place = lambda x, y, z, c: (y * 16 + (x // 2) * 8 + z * 2 + c) * 2 + x % 2
                    pairs.append((place(x, y, z, c), place(x2 % 4, y2 % 4, z2 % 4, c2)))
    return pairs


def send(value, where):
    return lax.ppermute(value, AXES, moved(where))


def swap_core(value):
    return send(value, lambda x, y, z, c: (x, y, z, 1 - c))


def swap_tp(value):
    return send(value, lambda x, y, z, c: (x ^ 1, y, z, c))


def send_cross(value, across, dz):
    return send(value, lambda x, y, z, c: (3 - x if across else x, y, z + dz, c))


def send_far(value, across, dz):
    return send(value, lambda x, y, z, c: (x + 2 * across, y, z + dz, c))


def send_pod(value, dy):
    return send(value, lambda x, y, z, c: (x, y + dy, z, c))


OTHERS = ((1, 2), (1, 1), (1, -1), (0, 2), (1, 0), (0, 1), (0, -1))


def normed(embed):
    e32 = embed.astype(F32)
    inverse = lax.rsqrt(jnp.sum(e32 * e32, axis=-1, keepdims=True) + EPS)
    return (e32 * inverse, inverse)


def embed_grad(z32, inverse, dz):
    return ((dz - z32 * jnp.sum(z32 * dz, axis=-1, keepdims=True)) * inverse).astype(BF16)


def body(
    img_embed,
    txt_embed,
    img_hidden,
    txt_hidden,
    proj_weights,
    residual_in,
    partner,
    group_ids,
    logit_scale,
    logit_bias,
    loss_scale,
):
    here = lax.axis_index("blk")
    tp = lax.axis_index("tp")
    x_hi, z, core = here // 8, (here // 2) % 4, here % 2
    half = tp ^ x_hi
    rows, width = img_embed.shape[1:]
    share = rows // 2
    pod = rows * lax.axis_size("blk")
    scale = logit_scale[0]
    bias = logit_bias[0]
    factor = loss_scale[0] / pod

    zt32, inv_t = normed(lax.dynamic_slice_in_dim(txt_embed[0], half * share, share, 0))
    texts = zt32.astype(BF16)
    gathered = {(0, 0): texts}
    for across, dz in OTHERS:
        gathered[across, dz] = send_cross(texts, across, dz)
    zi32, inv_i = normed(img_embed[0])
    own_images = zi32.astype(BF16)
    images = jnp.concatenate([own_images, swap_core(own_images)])
    ids = partner[0]
    other_ids = swap_tp(ids)
    ids = jnp.where(tp == 0, jnp.concatenate([ids, other_ids]), jnp.concatenate([other_ids, ids]))
    ids = jnp.concatenate([ids, swap_core(ids)])

    offsets = jnp.arange(share, dtype=jnp.int32)
    img_grad = None
    returned = []
    for (across, dz), block in gathered.items():
        chip = (x_hi ^ across) * 4 + (z - dz) % 4
        columns = (chip * 2 + core) * rows + half * share + offsets
        logits = (
            scale * jnp.einsum("ie,je->ij", images, block, preferred_element_type=F32) + bias
        )
        positive = (ids[:, None] == columns[None, :]).astype(F32)
        weights = ((jax.nn.sigmoid(logits) - positive) * factor).astype(BF16)
        to_img = jnp.einsum("ij,je->ie", weights, block, preferred_element_type=F32)
        to_txt = jnp.einsum("ij,ie->je", weights, images, preferred_element_type=F32)
        img_grad = to_img if img_grad is None else img_grad + to_img
        if (across, dz) == (0, 0):
            txt_grad = to_txt
        else:
            returned.append(send_cross(to_txt.astype(BF16), across, -dz))

    img_grad = img_grad[:rows] + swap_core(img_grad[rows:].astype(BF16)).astype(F32)
    img_grad = img_grad + swap_tp(img_grad.astype(BF16)).astype(F32)
    de_img = embed_grad(zi32, inv_i, scale * img_grad)

    for part in returned:
        txt_grad = txt_grad + part.astype(F32)
    de_half = embed_grad(zt32, inv_t, scale * txt_grad)
    de_other = swap_tp(de_half)
    de_txt = jnp.where(
        half == 0, jnp.concatenate([de_half, de_other]), jnp.concatenate([de_other, de_half])
    )

    outs, packs, residuals = [], [], []
    chip = x_hi * 4 + z
    for k, (de, hidden) in enumerate(((de_img, img_hidden[0]), (de_txt, txt_hidden[0]))):
        outs.append(
            jnp.einsum("re,fe->rf", de, proj_weights[k], preferred_element_type=F32).astype(BF16)
        )
        part = jnp.einsum("re,rf->ef", de, hidden, preferred_element_type=F32).astype(BF16)
        units = part.shape[1]
        part = part.reshape(8, 2, width // 16, units)
        got = swap_core(lax.dynamic_index_in_dim(part, 1 - core, 1, keepdims=False))
        mine = lax.dynamic_index_in_dim(part, core, 1, keepdims=False)

        def both(chip):
            return lax.dynamic_index_in_dim(mine, chip, 0, keepdims=False).astype(
                F32
            ) + lax.dynamic_index_in_dim(got, chip, 0, keepdims=False).astype(F32)

        grad = both(chip)
        for across, dz in OTHERS:
            target = (x_hi ^ across) * 4 + (z + dz) % 4
            grad = grad + send_far(both(target).astype(BF16), across, dz).astype(F32)
        g_total = grad + residual_in[0, :, k]
        onehot = (group_ids[k][None, :] == jnp.arange(NG, dtype=jnp.int32)[:, None]).astype(F32)
        absum = jnp.sum(jnp.abs(g_total), axis=0)
        group_total = jnp.sum(onehot * absum[None, :], axis=1)
        count = jnp.sum(onehot, axis=1) * g_total.shape[0]
        level = group_total / count + EPS
        spread = jnp.sum(onehot * level[:, None], axis=0)[None]
        packed = spread * jnp.tanh(g_total / spread)
        residuals.append(g_total - packed)
        p = packed.astype(BF16)
        up, down, far = send_pod(p, 1), send_pod(p, -1), send_pod(p, 2)
        packs.append((p.astype(F32) + far.astype(F32)) + (up.astype(F32) + down.astype(F32)))
    return (outs[0][None], outs[1][None], jnp.stack(packs, 1), jnp.stack(residuals, 1)[None])


def solution(mesh):
    placed = (
        P("outer", "blk", None),
        P("outer", "blk", None),
        P("outer", "blk", "tp"),
        P("outer", "blk", "tp"),
        P(None, "tp", None),
        P("outer", "blk", None, "tp"),
        P("outer", ("blk", "tp")),
        P(None, "tp"),
        P(),
        P(),
        P(),
    )
    return jax.shard_map(
        body,
        mesh=mesh,
        in_specs=placed,
        out_specs=(
            P("outer", "blk", "tp"),
            P("outer", "blk", "tp"),
            P("blk", None, "tp"),
            P("outer", "blk", None, "tp"),
        ),
        check_vma=False,
    )
```

```python
import jax
import jax.numpy as jnp
from jax import lax
from jax.sharding import PartitionSpec as P

NG = 8
EPS = 1e-06
AXES = ("outer", "blk", "tp")
F32 = jnp.float32
BF16 = jnp.bfloat16


def moved(where):
    pairs = []
    for y in range(4):
        for x in range(4):
            for z in range(4):
                for c in range(2):
                    x2, y2, z2, c2 = where(x, y, z, c)
                    place = lambda x, y, z, c: (y * 16 + (x // 2) * 8 + z * 2 + c) * 2 + x % 2
                    pairs.append((place(x, y, z, c), place(x2 % 4, y2 % 4, z2 % 4, c2)))
    return pairs


def send(value, where):
    return lax.ppermute(value, AXES, moved(where))


def swap_core(value):
    return send(value, lambda x, y, z, c: (x, y, z, 1 - c))


def swap_tp(value):
    return send(value, lambda x, y, z, c: (x ^ 1, y, z, c))


def send_cross(value, across, dz):
    return send(value, lambda x, y, z, c: (3 - x if across else x, y, z + dz, c))


def send_far(value, across, dz):
    return send(value, lambda x, y, z, c: (x + 2 * across, y, z + dz, c))


def send_pod(value, dy):
    return send(value, lambda x, y, z, c: (x, y + dy, z, c))


RING = (1, -1, 2)


def normed(embed):
    e32 = embed.astype(F32)
    inverse = lax.rsqrt(jnp.sum(e32 * e32, axis=-1, keepdims=True) + EPS)
    return (e32 * inverse, inverse)


def embed_grad(z32, inverse, dz):
    return ((dz - z32 * jnp.sum(z32 * dz, axis=-1, keepdims=True)) * inverse).astype(BF16)


def body(
    img_embed,
    txt_embed,
    img_hidden,
    txt_hidden,
    proj_weights,
    residual_in,
    partner,
    group_ids,
    logit_scale,
    logit_bias,
    loss_scale,
):
    here = lax.axis_index("blk")
    tp = lax.axis_index("tp")
    x_hi, z, core = here // 8, (here // 2) % 4, here % 2
    half = tp ^ x_hi
    rows, width = img_embed.shape[1:]
    share = rows // 2
    pod = rows * lax.axis_size("blk")
    scale = logit_scale[0]
    bias = logit_bias[0]
    factor = loss_scale[0] / pod

    zt32, inv_t = normed(lax.dynamic_slice_in_dim(txt_embed[0], half * share, share, 0))
    texts = zt32.astype(BF16)
    ids = partner[0]
    other_ids = swap_tp(ids)
    ids = jnp.where(tp == 0, jnp.concatenate([ids, other_ids]), jnp.concatenate([other_ids, ids]))
    ids = jnp.concatenate([ids, swap_core(ids)])

    quarter = share // 2
    low, high = texts[:quarter], texts[quarter:]
    low_cross = send_cross(low, 1, 0)
    high_ring = [send_cross(high, 0, dz) for dz in RING]
    zi32, inv_i = normed(img_embed[0])
    own_images = zi32.astype(BF16)
    images = jnp.concatenate([own_images, swap_core(own_images)])
    low_pair = jnp.concatenate([low, low_cross])
    low_ring = [send_cross(low_pair, 0, dz) for dz in RING]
    high_cross = send_cross(jnp.concatenate([high, *high_ring]), 1, 0)

    offsets = jnp.arange(quarter, dtype=jnp.int32)

    def column_ids(place):
        across, dz, start = place
        chip = (x_hi ^ across) * 4 + (z - dz) % 4
        return (chip * 2 + core) * rows + half * share + start + offsets

    def products(block, places):
        columns = jnp.concatenate([column_ids(place) for place in places])
        logits = (
            scale * jnp.einsum("ie,je->ij", images, block, preferred_element_type=F32) + bias
        )
        positive = (ids[:, None] == columns[None, :]).astype(F32)
        weights = ((jax.nn.sigmoid(logits) - positive) * factor).astype(BF16)
        to_txt = jnp.einsum("ij,ie->je", weights, images, preferred_element_type=F32)
        to_img = jnp.einsum("ij,je->ie", weights, block, preferred_element_type=F32)
        return to_txt, to_img

    near_txt, near_img = products(
        jnp.concatenate([low_pair, high, *high_ring]),
        [(0, 0, 0), (1, 0, 0), (0, 0, quarter)] + [(0, dz, quarter) for dz in RING],
    )
    far_txt, far_img = products(
        jnp.concatenate([*low_ring, high_cross]),
        [(across, dz, 0) for dz in RING for across in (0, 1)]
        + [(1, dz, quarter) for dz in (0,) + RING],
    )
    far_send = far_txt.astype(BF16)
    low_back = [
        send_cross(far_send[i * share : (i + 1) * share], 0, -dz) for i, dz in enumerate(RING)
    ]
    high_back = send_cross(far_send[3 * share :], 1, 0)
    img_grad = near_img + far_img

    img_grad = img_grad[:rows] + swap_core(img_grad[rows:].astype(BF16)).astype(F32)
    img_grad = img_grad + swap_tp(img_grad.astype(BF16)).astype(F32)
    de_img = embed_grad(zi32, inv_i, scale * img_grad)

    low_sum = near_txt[:share]
    for part in low_back:
        low_sum = low_sum + part.astype(F32)
    high_sum = near_txt[share:] + high_back.astype(F32)
    high_send = high_sum[quarter:].astype(BF16)
    low_last = send_cross(low_sum[quarter:].astype(BF16), 1, 0)
    high_last = [
        send_cross(high_send[i * quarter : (i + 1) * quarter], 0, -dz)
        for i, dz in enumerate(RING)
    ]
    _, low_last, *high_last = lax.optimization_barrier((de_img, low_last, *high_last))
    low_sum = low_sum[:quarter] + low_last.astype(F32)
    high_sum = high_sum[:quarter]
    for part in high_last:
        high_sum = high_sum + part.astype(F32)
    de_half = embed_grad(zt32, inv_t, scale * jnp.concatenate([low_sum, high_sum]))
    de_other = swap_tp(de_half)
    de_txt = jnp.where(
        half == 0, jnp.concatenate([de_half, de_other]), jnp.concatenate([de_other, de_half])
    )

    outs, packs, residuals = [], [], []
    for k, (de, hidden) in enumerate(((de_img, img_hidden[0]), (de_txt, txt_hidden[0]))):
        turned = de.T.reshape(8, 2, width // 16, rows)
        units = hidden.shape[1]

        def part(parity):
            chosen = lax.dynamic_index_in_dim(turned, parity, 1, keepdims=False)
            return jnp.einsum(
                "er,fr->ef", chosen.reshape(width // 2, rows), hidden.T, preferred_element_type=F32
            ).astype(BF16)

        got = swap_core(part(1 - core)).reshape(2, 4, width // 16, units)
        mine = part(core).reshape(2, 4, width // 16, units)

        def both(x_from, z_from, x_count, z_count, start, stop):
            sizes = (x_count, z_count, width // 16, stop - start)
            places = (x_from, z_from, 0, start)
            return lax.dynamic_slice(mine, places, sizes).astype(F32) + lax.dynamic_slice(
                got, places, sizes
            ).astype(F32)

        middle = units // 256 * 128
        last_cross = send_far(both(1 - x_hi, 0, 1, 4, middle, units).astype(BF16), 1, 0)
        first_ring = [
            send_far(both(0, (z + dz) % 4, 2, 1, 0, middle).astype(BF16), 0, dz) for dz in RING
        ]
        last = both(x_hi, 0, 1, 4, middle, units)[0] + last_cross[0].astype(F32)
        first = both(0, z, 2, 1, 0, middle)[:, 0]
        for piece in first_ring:
            first = first + piece[:, 0].astype(F32)
        last_ring = [
            send_far(
                lax.dynamic_index_in_dim(last, (z + dz) % 4, 0, keepdims=False).astype(BF16), 0, dz
            )
            for dz in RING
        ]
        first_cross = send_far(
            lax.dynamic_index_in_dim(first, 1 - x_hi, 0, keepdims=False).astype(BF16), 1, 0
        )
        late, _ = lax.optimization_barrier((de, last_cross))
        outs.append(
            jnp.einsum("re,fe->rf", late, proj_weights[k], preferred_element_type=F32).astype(BF16)
        )
        first = lax.dynamic_index_in_dim(first, x_hi, 0, keepdims=False) + first_cross.astype(F32)
        last = lax.dynamic_index_in_dim(last, z, 0, keepdims=False)
        for piece in last_ring:
            last = last + piece.astype(F32)
        grad = jnp.concatenate([first, last], axis=1)
        g_total = grad + residual_in[0, :, k]
        onehot = (group_ids[k][None, :] == jnp.arange(NG, dtype=jnp.int32)[:, None]).astype(F32)
        absum = jnp.sum(jnp.abs(g_total), axis=0)
        group_total = jnp.sum(onehot * absum[None, :], axis=1)
        count = jnp.sum(onehot, axis=1) * g_total.shape[0]
        level = group_total / count + EPS
        spread = jnp.sum(onehot * level[:, None], axis=0)[None]
        packed = spread * jnp.tanh(g_total / spread)
        residuals.append(g_total - packed)
        p = packed.astype(BF16)
        up, down, far = send_pod(p, 1), send_pod(p, -1), send_pod(p, 2)
        packs.append((p.astype(F32) + far.astype(F32)) + (up.astype(F32) + down.astype(F32)))
    return (outs[0][None], outs[1][None], jnp.stack(packs, 1), jnp.stack(residuals, 1)[None])


def solution(mesh):
    placed = (
        P("outer", "blk", None),
        P("outer", "blk", None),
        P("outer", "blk", "tp"),
        P("outer", "blk", "tp"),
        P(None, "tp", None),
        P("outer", "blk", None, "tp"),
        P("outer", ("blk", "tp")),
        P(None, "tp"),
        P(),
        P(),
        P(),
    )
    return jax.shard_map(
        body,
        mesh=mesh,
        in_specs=placed,
        out_specs=(
            P("outer", "blk", "tp"),
            P("outer", "blk", "tp"),
            P("blk", None, "tp"),
            P("outer", "blk", None, "tp"),
        ),
        check_vma=False,
    )
```

```python
import jax
import jax.numpy as jnp
from jax import lax
from jax.experimental import pallas as pl
from jax.experimental.pallas import tpu as pltpu
from jax.sharding import PartitionSpec as P

NG = 8
EPS = 1e-06
AXES = ("outer", "blk", "tp")
F32 = jnp.float32
BF16 = jnp.bfloat16


def moved(where):
    pairs = []
    for y in range(4):
        for x in range(4):
            for z in range(4):
                for c in range(2):
                    x2, y2, z2, c2 = where(x, y, z, c)
                    place = lambda x, y, z, c: (y * 16 + (x // 2) * 8 + z * 2 + c) * 2 + x % 2
                    pairs.append((place(x, y, z, c), place(x2 % 4, y2 % 4, z2 % 4, c2)))
    return pairs


def send(value, where):
    return lax.ppermute(value, AXES, moved(where))


def swap_core(value):
    return send(value, lambda x, y, z, c: (x, y, z, 1 - c))


def swap_tp(value):
    return send(value, lambda x, y, z, c: (x ^ 1, y, z, c))


def send_cross(value, across, dz):
    return send(value, lambda x, y, z, c: (3 - x if across else x, y, z + dz, c))


def send_far(value, across, dz):
    return send(value, lambda x, y, z, c: (x + 2 * across, y, z + dz, c))


def send_pod(value, dy):
    return send(value, lambda x, y, z, c: (x, y + dy, z, c))


RING = (1, -1, 2)
DIGIT = 64


class Line:
    def __init__(self):
        self.marked = ()

    def ready(self, *values):
        values = lax.optimization_barrier((*values, *self.marked))[: len(values)]
        return values[0] if len(values) == 1 else values

    def mark(self, *values):
        self.marked = values


def split_grad_kernel(core, de, hidden, mine, other, turned):
    half = turned.shape[0] // 2

    @pl.when(pl.program_id(0) == 0)
    def _():
        flat = de[...].astype(F32).T
        rows = flat.shape[0] // 16
        pieces = [flat[i * rows : (i + 1) * rows] for i in range(16)]
        even, odd = jnp.concatenate(pieces[0::2]), jnp.concatenate(pieces[1::2])
        first = core[0] == 0
        turned[:half] = jnp.where(first, even, odd).astype(BF16)
        turned[half:] = jnp.where(first, odd, even).astype(BF16)

    for out, rows in ((mine, slice(0, half)), (other, slice(half, None))):
        out[...] = lax.dot_general(
            turned[rows], hidden[...], (((1,), (1,)), ((), ())), preferred_element_type=F32
        ).astype(BF16)


def split_grad(core, de, hidden):
    rows, width = de.shape
    units = hidden.shape[1]
    tile = 512
    block = pl.BlockSpec((width // 2, tile), lambda i: (0, i))
    return pl.pallas_call(
        split_grad_kernel,
        grid=(pl.cdiv(units, tile),),
        in_specs=[
            pl.BlockSpec(memory_space=pltpu.SMEM),
            pl.BlockSpec((rows, width), lambda i: (0, 0)),
            pl.BlockSpec((tile, rows), lambda i: (i, 0)),
        ],
        out_specs=[block, block],
        out_shape=[jax.ShapeDtypeStruct((width // 2, units), BF16)] * 2,
        scratch_shapes=[pltpu.VMEM((width, rows), BF16)],
        cost_estimate=pl.CostEstimate(flops=1024, bytes_accessed=1024, transcendentals=0),
        compiler_params=pltpu.CompilerParams(vmem_limit_bytes=24 * 1024 * 1024),
        name="split_grad",
    )(jnp.reshape(core, (1,)), de, hidden.T)


def hidden_grad_kernel(weights, de, out):
    out[...] = lax.dot_general(
        weights[...], de[...], (((1,), (1,)), ((), ())), preferred_element_type=F32
    ).astype(BF16)


def hidden_grad(weights, k, de):
    rows, width = de.shape
    units = weights.shape[1]
    tile = 544
    return pl.pallas_call(
        hidden_grad_kernel,
        grid=(pl.cdiv(units, tile),),
        in_specs=[
            pl.BlockSpec((None, tile, width), lambda i: (k, i, 0)),
            pl.BlockSpec((rows, width), lambda i: (0, 0)),
        ],
        out_specs=pl.BlockSpec((tile, rows), lambda i: (i, 0)),
        out_shape=jax.ShapeDtypeStruct((units, rows), BF16),
        cost_estimate=pl.CostEstimate(flops=1024, bytes_accessed=1024, transcendentals=0),
        compiler_params=pltpu.CompilerParams(vmem_limit_bytes=24 * 1024 * 1024),
        name="hidden_grad",
    )(weights, de)


def normed(embed):
    e32 = embed.astype(F32)
    inverse = lax.rsqrt(jnp.sum(e32 * e32, axis=-1, keepdims=True) + EPS)
    return (e32 * inverse, inverse)


def embed_grad(z32, inverse, dz):
    return ((dz - z32 * jnp.sum(z32 * dz, axis=-1, keepdims=True)) * inverse).astype(BF16)


def body(
    img_embed,
    txt_embed,
    img_hidden,
    txt_hidden,
    proj_weights,
    residual_in,
    partner,
    group_ids,
    logit_scale,
    logit_bias,
    loss_scale,
):
    here = lax.axis_index("blk")
    tp = lax.axis_index("tp")
    x_hi, z, core = here // 8, (here // 2) % 4, here % 2
    half = tp ^ x_hi
    rows, width = img_embed.shape[1:]
    share, quarter = rows // 2, rows // 4
    pod = rows * lax.axis_size("blk")
    scale = logit_scale[0]
    bias = logit_bias[0]
    factor = loss_scale[0] / pod
    line = Line()

    ids = partner[0]
    other_ids = swap_tp(ids)
    zt32, inv_t = normed(lax.dynamic_slice_in_dim(txt_embed[0], half * share, share, 0))
    texts = zt32.astype(BF16)
    line.mark(texts)
    low, high = texts[:quarter], texts[quarter:]
    low_cross = send_cross(low, 1, 0)
    high_ring = [send_cross(high, 0, dz) for dz in RING]

    img, other_ids = line.ready(img_embed[0], other_ids)
    ids = jnp.where(tp == 0, jnp.concatenate([ids, other_ids]), jnp.concatenate([other_ids, ids]))
    zi32, inv_i = normed(img)
    digits = jnp.stack([ids // DIGIT, ids % DIGIT]).astype(BF16)
    digits = jnp.pad(digits, ((0, 14), (0, width - rows)))
    own_images = jnp.concatenate([zi32.astype(BF16), digits])
    line.mark(own_images)
    core_images = swap_core(own_images)

    low_pair = jnp.concatenate(line.ready(low, low_cross))
    line.mark(low_pair)
    low_ring = [send_cross(low_pair, 0, dz) for dz in RING]
    high_all = jnp.concatenate(line.ready(high, *high_ring))
    line.mark(high_all)
    high_cross = send_cross(high_all, 1, 0)
    core_images = line.ready(core_images)
    images = jnp.concatenate([own_images[:rows], core_images[:rows]])
    digits = core_images[rows : rows + 2, :rows].astype(jnp.int32)
    ids = jnp.concatenate([ids, digits[0] * DIGIT + digits[1]])
    offsets = jnp.arange(quarter, dtype=jnp.int32)

    def column_ids(place):
        across, dz, start = place
        chip = (x_hi ^ across) * 4 + (z - dz) % 4
        return (chip * 2 + core) * rows + half * share + start + offsets

    def products(block, places):
        columns = jnp.concatenate([column_ids(place) for place in places])
        logits = (
            scale * jnp.einsum("ie,je->ij", images, block, preferred_element_type=F32) + bias
        )
        positive = (ids[:, None] == columns[None, :]).astype(F32)
        weights = ((jax.nn.sigmoid(logits) - positive) * factor).astype(BF16)
        to_txt = jnp.einsum("ij,ie->je", weights, images, preferred_element_type=F32)
        return to_txt, weights

    def to_images(weights, block):
        return jnp.einsum("ij,je->ie", weights, block, preferred_element_type=F32)

    block = jnp.concatenate([low_pair, high_all])
    near_txt, weights = products(
        block, [(0, 0, 0), (1, 0, 0), (0, 0, quarter)] + [(0, dz, quarter) for dz in RING]
    )
    near_img = to_images(weights, block)
    line.mark(near_txt, near_img)
    block = jnp.concatenate(line.ready(*low_ring, high_cross))
    far_txt, weights = products(
        block,
        [(across, dz, 0) for dz in RING for across in (0, 1)]
        + [(1, dz, quarter) for dz in (0,) + RING],
    )
    far_send = far_txt.astype(BF16)
    line.mark(far_send)
    high_back = send_cross(far_send[3 * share :], 1, 0)
    low_back = [
        send_cross(far_send[i * share : (i + 1) * share], 0, -dz) for i, dz in enumerate(RING)
    ]

    img_grad = near_img + to_images(line.ready(weights), block)
    img_core = img_grad[rows:].astype(BF16)
    line.mark(img_core)
    img_grad = img_grad[:rows] + line.ready(swap_core(img_core)).astype(F32)
    img_send = img_grad.astype(BF16)
    line.mark(img_send)
    img_other = swap_tp(img_send)

    high_back, *low_back = line.ready(high_back, *low_back)
    low_sum = near_txt[:share]
    for part in low_back:
        low_sum = low_sum + part.astype(F32)
    high_sum = near_txt[share:] + high_back.astype(F32)
    low_send = low_sum[quarter:].astype(BF16)
    high_send = high_sum[quarter:].astype(BF16)
    line.mark(low_send, high_send)
    low_last = send_cross(low_send, 1, 0)
    high_last = [
        send_cross(high_send[i * quarter : (i + 1) * quarter], 0, -dz)
        for i, dz in enumerate(RING)
    ]

    units = img_hidden.shape[2]
    tiles = (2, 4, width // 16, units)

    def pick(value, i):
        return lax.dynamic_index_in_dim(value, i, 0, keepdims=False)

    def both(split, x_from, z_from, x_count, z_count):
        sizes = (x_count, z_count, width // 16, units)
        places = (x_from, z_from, 0, 0)
        mine, got = split
        return lax.dynamic_slice(mine, places, sizes).astype(F32) + lax.dynamic_slice(
            got, places, sizes
        ).astype(F32)

    img_grad = img_grad + line.ready(img_other).astype(F32)
    de_img = embed_grad(zi32, inv_i, scale * img_grad)
    img_mine, img_other = split_grad(core, de_img, img_hidden[0])
    line.mark(img_mine)
    img_got = swap_core(img_other)

    low_last, *high_last = line.ready(low_last, *high_last)
    low_sum = low_sum[:quarter] + low_last.astype(F32)
    high_sum = high_sum[:quarter]
    for part in high_last:
        high_sum = high_sum + part.astype(F32)
    de_half = embed_grad(zt32, inv_t, scale * jnp.concatenate([low_sum, high_sum]))
    line.mark(de_half)
    de_other = swap_tp(de_half)

    img_split = (img_mine.reshape(tiles), line.ready(img_got).reshape(tiles))
    leave = [both(img_split, 0, (z + dz) % 4, 2, 1).astype(BF16) for dz in RING]
    line.mark(*leave)
    img_parts = [send_far(value, 0, dz) for value, dz in zip(leave, RING)]

    de_half, de_other = line.ready(de_half, de_other)
    de_txt = jnp.where(
        half == 0, jnp.concatenate([de_half, de_other]), jnp.concatenate([de_other, de_half])
    )
    txt_mine, txt_other = split_grad(core, de_txt, txt_hidden[0])
    line.mark(txt_mine)
    txt_got = swap_core(txt_other)

    txt_split = (txt_mine.reshape(tiles), line.ready(txt_got).reshape(tiles))
    leave = both(txt_split, 1 - x_hi, 0, 1, 4).astype(BF16)
    line.mark(leave)
    txt_cross = send_far(leave, 1, 0)
    d_img = hidden_grad(proj_weights, 0, line.ready(de_img))
    line.mark(d_img)

    sums = both(img_split, 0, z, 2, 1)[:, 0]
    for part in line.ready(*img_parts):
        sums = sums + part[:, 0].astype(F32)
    grad_img = pick(sums, x_hi)
    leave = pick(sums, 1 - x_hi).astype(BF16)
    line.mark(leave)
    img_cross = send_far(leave, 1, 0)

    sums = both(txt_split, x_hi, 0, 1, 4)[0] + line.ready(txt_cross)[0].astype(F32)
    grad_txt = pick(sums, z)
    leave = [pick(sums, (z + dz) % 4).astype(BF16) for dz in RING]
    line.mark(*leave)
    txt_parts = [send_far(value, 0, dz) for value, dz in zip(leave, RING)]

    onehots = [
        (group_ids[k][None, :] == jnp.arange(NG, dtype=jnp.int32)[:, None]).astype(F32)
        for k in range(2)
    ]
    counts = [jnp.sum(onehot, axis=1) * residual_in.shape[1] for onehot in onehots]

    def packed_of(g_total, k):
        absum = jnp.sum(jnp.abs(g_total), axis=0)
        group_total = jnp.sum(onehots[k] * absum[None, :], axis=1)
        level = group_total / counts[k] + EPS
        spread = jnp.sum(onehots[k] * level[:, None], axis=0)[None]
        return spread * jnp.tanh(g_total / spread)

    def pods(packed):
        return [packed, send_pod(packed, 2), send_pod(packed, 1), send_pod(packed, -1)]

    def pod_sum(parts):
        own, far, up, down = (part.astype(F32) for part in parts)
        return (own + far) + (up + down)

    g_img = grad_img + line.ready(img_cross).astype(F32) + residual_in[0, :, 0]
    packed_img = packed_of(g_img, 0)
    img_pods = pods(packed_img.astype(BF16))
    line.mark(img_pods[0])
    d_txt = hidden_grad(proj_weights, 1, line.ready(de_txt))
    line.mark(d_txt)
    for part in line.ready(*txt_parts):
        grad_txt = grad_txt + part.astype(F32)
    g_txt = grad_txt + residual_in[0, :, 1]
    packed_txt = packed_of(g_txt, 1)
    txt_pods = pods(packed_txt.astype(BF16))
    line.mark(txt_pods[0])
    sum_img = pod_sum(line.ready(*img_pods))
    line.mark(sum_img)
    residual = jnp.stack([g_img - packed_img, g_txt - packed_txt], 1)
    summed = jnp.stack([sum_img, pod_sum(line.ready(*txt_pods))], 1)
    return (d_img.T[None], d_txt.T[None], summed, residual[None])


def solution(mesh):
    placed = (
        P("outer", "blk", None),
        P("outer", "blk", None),
        P("outer", "blk", "tp"),
        P("outer", "blk", "tp"),
        P(None, "tp", None),
        P("outer", "blk", None, "tp"),
        P("outer", ("blk", "tp")),
        P(None, "tp"),
        P(),
        P(),
        P(),
    )
    return jax.shard_map(
        body,
        mesh=mesh,
        in_specs=placed,
        out_specs=(
            P("outer", "blk", "tp"),
            P("outer", "blk", "tp"),
            P("blk", None, "tp"),
            P("outer", "blk", None, "tp"),
        ),
        check_vma=False,
    )
```

```python
import jax
import jax.numpy as jnp
from jax import lax
from jax.experimental import pallas as pl
from jax.experimental.pallas import tpu as pltpu
from jax.sharding import PartitionSpec as P

NG = 8
EPS = 1e-06
AXES = ("outer", "blk", "tp")
F32 = jnp.float32
BF16 = jnp.bfloat16


def moved(where):
    pairs = []
    for y in range(4):
        for x in range(4):
            for z in range(4):
                for c in range(2):
                    x2, y2, z2, c2 = where(x, y, z, c)
                    place = lambda x, y, z, c: (y * 16 + (x // 2) * 8 + z * 2 + c) * 2 + x % 2
                    pairs.append((place(x, y, z, c), place(x2 % 4, y2 % 4, z2 % 4, c2)))
    return pairs


def send(value, where):
    return lax.ppermute(value, AXES, moved(where))


def swap_core(value):
    return send(value, lambda x, y, z, c: (x, y, z, 1 - c))


def swap_tp(value):
    return send(value, lambda x, y, z, c: (x ^ 1, y, z, c))


def send_cross(value, across, dz):
    return send(value, lambda x, y, z, c: (3 - x if across else x, y, z + dz, c))


def send_far(value, across, dz):
    return send(value, lambda x, y, z, c: (x + 2 * across, y, z + dz, c))


def send_pod(value, dy):
    return send(value, lambda x, y, z, c: (x, y + dy, z, c))


RING = (1, -1, 2)
DIGIT = 64


class Line:
    def __init__(self):
        self.marked = ()

    def ready(self, *values):
        values = lax.optimization_barrier((*values, *self.marked))[: len(values)]
        return values[0] if len(values) == 1 else values

    def mark(self, *values):
        self.marked = values


def split_grad_kernel(core, de, hidden, mine, other, turned):
    half = turned.shape[0] // 2

    @pl.when(pl.program_id(0) == 0)
    def _():
        flat = de[...].astype(F32).T
        rows = flat.shape[0] // 16
        pieces = [flat[i * rows : (i + 1) * rows] for i in range(16)]
        even, odd = jnp.concatenate(pieces[0::2]), jnp.concatenate(pieces[1::2])
        first = core[0] == 0
        turned[:half] = jnp.where(first, even, odd).astype(BF16)
        turned[half:] = jnp.where(first, odd, even).astype(BF16)

    for out, rows in ((mine, slice(0, half)), (other, slice(half, None))):
        out[...] = lax.dot_general(
            turned[rows], hidden[...], (((1,), (1,)), ((), ())), preferred_element_type=F32
        ).astype(BF16)


def split_grad(core, de, hidden):
    rows, width = de.shape
    units = hidden.shape[1]
    tile = 1152
    block = pl.BlockSpec((width // 2, tile), lambda i: (0, i))
    return pl.pallas_call(
        split_grad_kernel,
        grid=(pl.cdiv(units, tile),),
        in_specs=[
            pl.BlockSpec(memory_space=pltpu.SMEM),
            pl.BlockSpec((rows, width), lambda i: (0, 0)),
            pl.BlockSpec((tile, rows), lambda i: (i, 0)),
        ],
        out_specs=[block, block],
        out_shape=[pltpu.HBM((width // 2, units), BF16)] * 2,
        scratch_shapes=[pltpu.VMEM((width, rows), BF16)],
        cost_estimate=pl.CostEstimate(flops=1024, bytes_accessed=1024, transcendentals=0),
        compiler_params=pltpu.CompilerParams(vmem_limit_bytes=16 * 1024 * 1024),
        name="split_grad",
    )(jnp.reshape(core, (1,)), de, hidden.T)


def hidden_grad_kernel(weights, de, out):
    out[...] = lax.dot_general(
        weights[...], de[...], (((1,), (1,)), ((), ())), preferred_element_type=F32
    ).astype(BF16)


def hidden_grad(weights, k, de):
    rows, width = de.shape
    units = weights.shape[1]
    tile = 1088
    return pl.pallas_call(
        hidden_grad_kernel,
        grid=(pl.cdiv(units, tile),),
        in_specs=[
            pl.BlockSpec((None, tile, width), lambda i: (k, i, 0)),
            pl.BlockSpec((rows, width), lambda i: (0, 0)),
        ],
        out_specs=pl.BlockSpec((tile, rows), lambda i: (i, 0)),
        out_shape=jax.ShapeDtypeStruct((units, rows), BF16),
        cost_estimate=pl.CostEstimate(flops=1024, bytes_accessed=1024, transcendentals=0),
        compiler_params=pltpu.CompilerParams(vmem_limit_bytes=12 * 1024 * 1024),
        name="hidden_grad",
    )(weights, de)


def normed(embed):
    e32 = embed.astype(F32)
    inverse = lax.rsqrt(jnp.sum(e32 * e32, axis=-1, keepdims=True) + EPS)
    return (e32 * inverse, inverse)


def embed_grad(z32, inverse, dz):
    return ((dz - z32 * jnp.sum(z32 * dz, axis=-1, keepdims=True)) * inverse).astype(BF16)


def body(
    img_embed,
    txt_embed,
    img_hidden,
    txt_hidden,
    proj_weights,
    residual_in,
    partner,
    group_ids,
    logit_scale,
    logit_bias,
    loss_scale,
):
    here = lax.axis_index("blk")
    tp = lax.axis_index("tp")
    x_hi, z, core = here // 8, (here // 2) % 4, here % 2
    half = tp ^ x_hi
    rows, width = img_embed.shape[1:]
    share, quarter = rows // 2, rows // 4
    pod = rows * lax.axis_size("blk")
    scale = logit_scale[0]
    bias = logit_bias[0]
    factor = loss_scale[0] / pod
    line = Line()

    ids = partner[0]
    other_ids = swap_tp(ids)
    zt32, inv_t = normed(lax.dynamic_slice_in_dim(txt_embed[0], half * share, share, 0))
    texts = zt32.astype(BF16)
    line.mark(texts)
    low, high = texts[:quarter], texts[quarter:]
    low_cross = send_cross(low, 1, 0)
    high_ring = [send_cross(high, 0, dz) for dz in RING]

    img, other_ids = line.ready(img_embed[0], other_ids)
    ids = jnp.where(tp == 0, jnp.concatenate([ids, other_ids]), jnp.concatenate([other_ids, ids]))
    zi32, inv_i = normed(img)
    digits = jnp.stack([ids // DIGIT, ids % DIGIT]).astype(BF16)
    digits = jnp.pad(digits, ((0, 14), (0, width - rows)))
    own_images = jnp.concatenate([zi32.astype(BF16), digits])
    line.mark(own_images)
    core_images = swap_core(own_images)

    low_pair = jnp.concatenate(line.ready(low, low_cross))
    line.mark(low_pair)
    low_ring = [send_cross(low_pair, 0, dz) for dz in RING]
    high_all = jnp.concatenate(line.ready(high, *high_ring))
    line.mark(high_all)
    high_cross = send_cross(high_all, 1, 0)
    core_images = line.ready(core_images)
    images = jnp.concatenate([own_images[:rows], core_images[:rows]])
    digits = core_images[rows : rows + 2, :rows].astype(jnp.int32)
    ids = jnp.concatenate([ids, digits[0] * DIGIT + digits[1]])
    offsets = jnp.arange(quarter, dtype=jnp.int32)

    def column_ids(place):
        across, dz, start = place
        chip = (x_hi ^ across) * 4 + (z - dz) % 4
        return (chip * 2 + core) * rows + half * share + start + offsets

    def products(block, places):
        columns = jnp.concatenate([column_ids(place) for place in places])
        logits = (
            scale * jnp.einsum("ie,je->ij", images, block, preferred_element_type=F32) + bias
        )
        positive = (ids[:, None] == columns[None, :]).astype(F32)
        weights = ((jax.nn.sigmoid(logits) - positive) * factor).astype(BF16)
        to_txt = jnp.einsum("ij,ie->je", weights, images, preferred_element_type=F32)
        return to_txt, weights

    def to_images(weights, block):
        return jnp.einsum("ij,je->ie", weights, block, preferred_element_type=F32)

    block = jnp.concatenate([low_pair, high_all])
    near_txt, weights = products(
        block, [(0, 0, 0), (1, 0, 0), (0, 0, quarter)] + [(0, dz, quarter) for dz in RING]
    )
    near_img = to_images(weights, block)
    line.mark(near_txt, near_img)
    block = jnp.concatenate(line.ready(*low_ring, high_cross))
    far_txt, weights = products(
        block,
        [(across, dz, 0) for dz in RING for across in (0, 1)]
        + [(1, dz, quarter) for dz in (0,) + RING],
    )
    far_send = far_txt.astype(BF16)
    line.mark(far_send)
    high_back = send_cross(far_send[3 * share :], 1, 0)
    low_back = [
        send_cross(far_send[i * share : (i + 1) * share], 0, -dz) for i, dz in enumerate(RING)
    ]

    img_grad = near_img + to_images(line.ready(weights), block)
    img_core = img_grad[rows:].astype(BF16)
    line.mark(img_core)
    img_grad = img_grad[:rows] + line.ready(swap_core(img_core)).astype(F32)
    img_send = img_grad.astype(BF16)
    line.mark(img_send)
    img_other = swap_tp(img_send)

    img_other, high_back, *low_back = line.ready(img_other, high_back, *low_back)

    def low_part(i, near_txt, low_back):
        total = near_txt[i * quarter : (i + 1) * quarter]
        for part in low_back:
            total = total + part[i * quarter : (i + 1) * quarter].astype(F32)
        return total

    def high_part(i, near_txt, high_back):
        here = slice(i * quarter, (i + 1) * quarter)
        return near_txt[share:][here] + high_back[here].astype(F32)

    low_send = low_part(1, near_txt, low_back).astype(BF16)
    high_send = [high_part(i, near_txt, high_back).astype(BF16) for i in (1, 2, 3)]
    line.mark(low_send, *high_send)
    low_last = send_cross(low_send, 1, 0)
    high_last = [send_cross(value, 0, -dz) for value, dz in zip(high_send, RING)]

    units = img_hidden.shape[2]
    tiles = (2, 4, width // 16, units)

    def pick(value, i):
        return lax.dynamic_index_in_dim(value, i, 0, keepdims=False)

    def both(split, x_from, z_from, x_count, z_count):
        sizes = (x_count, z_count, width // 16, units)
        places = (x_from, z_from, 0, 0)
        mine, got = split
        return lax.dynamic_slice(mine, places, sizes).astype(F32) + lax.dynamic_slice(
            got, places, sizes
        ).astype(F32)

    near_txt, high_back, low_last, *parts = line.ready(
        near_txt, high_back, low_last, *low_back, *high_last
    )
    low_sum = low_part(0, near_txt, parts[:3]) + low_last.astype(F32)
    high_sum = high_part(0, near_txt, high_back)
    for part in parts[3:]:
        high_sum = high_sum + part.astype(F32)
    de_half = embed_grad(zt32, inv_t, scale * jnp.concatenate([low_sum, high_sum]))
    line.mark(de_half)
    de_other = swap_tp(de_half)

    img_grad = img_grad + line.ready(img_other).astype(F32)
    de_img = embed_grad(zi32, inv_i, scale * img_grad)
    line.mark(de_img)
    de_half, de_other = line.ready(de_half, de_other)
    de_txt = jnp.where(
        half == 0, jnp.concatenate([de_half, de_other]), jnp.concatenate([de_other, de_half])
    )
    txt_mine, txt_other = split_grad(core, de_txt, txt_hidden[0])
    line.mark(txt_other)
    txt_got = swap_core(txt_other)
    img_mine, img_other = split_grad(core, line.ready(de_img), img_hidden[0])
    line.mark(img_other)
    img_got = swap_core(img_other)

    txt_split = (txt_mine.reshape(tiles), line.ready(txt_got).reshape(tiles))
    leave = [both(txt_split, 0, (z + dz) % 4, 2, 1).astype(BF16) for dz in RING]
    line.mark(*leave)
    txt_parts = [send_far(value, 0, dz) for value, dz in zip(leave, RING)]
    img_split = (img_mine.reshape(tiles), line.ready(img_got).reshape(tiles))
    leave = both(img_split, 1 - x_hi, 0, 1, 4).astype(BF16)
    line.mark(leave)
    img_cross = send_far(leave, 1, 0)
    d_txt = hidden_grad(proj_weights, 1, line.ready(de_txt))
    line.mark(d_txt)
    d_img = hidden_grad(proj_weights, 0, line.ready(de_img))
    line.mark(d_img)

    sums = both(txt_split, 0, z, 2, 1)[:, 0]
    for part in line.ready(*txt_parts):
        sums = sums + part[:, 0].astype(F32)
    grad_txt = pick(sums, x_hi)
    leave = pick(sums, 1 - x_hi).astype(BF16)
    line.mark(leave)
    txt_cross = send_far(leave, 1, 0)

    sums = both(img_split, x_hi, 0, 1, 4)[0] + line.ready(img_cross)[0].astype(F32)
    grad_img = pick(sums, z)
    leave = [pick(sums, (z + dz) % 4).astype(BF16) for dz in RING]
    line.mark(*leave)
    img_parts = [send_far(value, 0, dz) for value, dz in zip(leave, RING)]

    onehots = [
        (group_ids[k][None, :] == jnp.arange(NG, dtype=jnp.int32)[:, None]).astype(F32)
        for k in range(2)
    ]
    counts = [jnp.sum(onehot, axis=1) * residual_in.shape[1] for onehot in onehots]

    def packed_of(g_total, k):
        absum = jnp.sum(jnp.abs(g_total), axis=0)
        group_total = jnp.sum(onehots[k] * absum[None, :], axis=1)
        level = group_total / counts[k] + EPS
        spread = jnp.sum(onehots[k] * level[:, None], axis=0)[None]
        return spread * jnp.tanh(g_total / spread)

    def pods(packed):
        return [packed, send_pod(packed, 2), send_pod(packed, 1), send_pod(packed, -1)]

    def pod_sum(parts):
        own, far, up, down = (part.astype(F32) for part in parts)
        return (own + far) + (up + down)

    g_txt = grad_txt + line.ready(txt_cross).astype(F32) + residual_in[0, :, 1]
    packed_txt = packed_of(g_txt, 1)
    txt_pods = pods(packed_txt.astype(BF16))
    line.mark(txt_pods[0])
    for part in line.ready(*img_parts):
        grad_img = grad_img + part.astype(F32)
    g_img = grad_img + residual_in[0, :, 0]
    packed_img = packed_of(g_img, 0)
    img_pods = pods(packed_img.astype(BF16))
    line.mark(img_pods[0])
    sum_txt = pod_sum(line.ready(*txt_pods))
    line.mark(sum_txt)
    residual = jnp.stack([g_img - packed_img, g_txt - packed_txt], 1)
    summed = jnp.stack([pod_sum(line.ready(*img_pods)), sum_txt], 1)
    return (d_img.T[None], d_txt.T[None], summed, residual[None])


def solution(mesh):
    placed = (
        P("outer", "blk", None),
        P("outer", "blk", None),
        P("outer", "blk", "tp"),
        P("outer", "blk", "tp"),
        P(None, "tp", None),
        P("outer", "blk", None, "tp"),
        P("outer", ("blk", "tp")),
        P(None, "tp"),
        P(),
        P(),
        P(),
    )
    return jax.shard_map(
        body,
        mesh=mesh,
        in_specs=placed,
        out_specs=(
            P("outer", "blk", "tp"),
            P("outer", "blk", "tp"),
            P("blk", None, "tp"),
            P("outer", "blk", None, "tp"),
        ),
        check_vma=False,
    )
```

```python
import jax
import jax.numpy as jnp
from jax import lax
from jax.experimental import pallas as pl
from jax.experimental.pallas import tpu as pltpu
from jax.sharding import PartitionSpec as P

NG = 8
EPS = 1e-06
AXES = ("outer", "blk", "tp")
F32 = jnp.float32
BF16 = jnp.bfloat16


def moved(where):
    pairs = []
    for y in range(4):
        for x in range(4):
            for z in range(4):
                for c in range(2):
                    x2, y2, z2, c2 = where(x, y, z, c)
                    place = lambda x, y, z, c: (y * 16 + (x // 2) * 8 + z * 2 + c) * 2 + x % 2
                    pairs.append((place(x, y, z, c), place(x2 % 4, y2 % 4, z2 % 4, c2)))
    return pairs


def send(value, where):
    return lax.ppermute(value, AXES, moved(where))


def swap_core(value):
    return send(value, lambda x, y, z, c: (x, y, z, 1 - c))


def swap_tp(value):
    return send(value, lambda x, y, z, c: (x ^ 1, y, z, c))


def send_cross(value, across, dz):
    return send(value, lambda x, y, z, c: (3 - x if across else x, y, z ^ dz, c))


def send_far(value, across, dz):
    return send(value, lambda x, y, z, c: (x + 2 * across, y, z ^ dz, c))


def send_pod(value, dy):
    return send(value, lambda x, y, z, c: (x, y ^ dy, z, c))


RING = (1, 3, 2)
DIGIT = 64


class Line:
    def __init__(self):
        self.marked = ()

    def ready(self, *values):
        values = lax.optimization_barrier((*values, *self.marked))[: len(values)]
        return values[0] if len(values) == 1 else values

    def mark(self, *values):
        self.marked = values


def split_grad_kernel(core, de, hidden, mine, other, turned):
    half = turned.shape[0] // 2

    @pl.when(pl.program_id(0) == 0)
    def _():
        flat = de[...].astype(F32).T
        rows = flat.shape[0] // 16
        pieces = [flat[i * rows : (i + 1) * rows] for i in range(16)]
        even, odd = jnp.concatenate(pieces[0::2]), jnp.concatenate(pieces[1::2])
        first = core[0] == 0
        turned[:half] = jnp.where(first, even, odd).astype(BF16)
        turned[half:] = jnp.where(first, odd, even).astype(BF16)

    for out, rows in ((mine, slice(0, half)), (other, slice(half, None))):
        out[...] = lax.dot_general(
            turned[rows], hidden[...], (((1,), (1,)), ((), ())), preferred_element_type=F32
        ).astype(BF16)


def split_grad(core, de, hidden):
    rows, width = de.shape
    units = hidden.shape[1]
    tile = 1152
    block = pl.BlockSpec((width // 2, tile), lambda i: (0, i))
    return pl.pallas_call(
        split_grad_kernel,
        grid=(pl.cdiv(units, tile),),
        in_specs=[
            pl.BlockSpec(memory_space=pltpu.SMEM),
            pl.BlockSpec((rows, width), lambda i: (0, 0)),
            pl.BlockSpec((tile, rows), lambda i: (i, 0)),
        ],
        out_specs=[block, block],
        out_shape=[pltpu.HBM((width // 2, units), BF16)] * 2,
        scratch_shapes=[pltpu.VMEM((width, rows), BF16)],
        cost_estimate=pl.CostEstimate(flops=1024, bytes_accessed=1024, transcendentals=0),
        compiler_params=pltpu.CompilerParams(vmem_limit_bytes=16 * 1024 * 1024),
        name="split_grad",
    )(jnp.reshape(core, (1,)), de, hidden.T)


def hidden_grad_kernel(weights, de, out):
    out[...] = lax.dot_general(
        weights[...], de[...], (((1,), (1,)), ((), ())), preferred_element_type=F32
    ).astype(BF16)


def hidden_grad(weights, k, de):
    rows, width = de.shape
    units = weights.shape[1]
    tile = 1088
    return pl.pallas_call(
        hidden_grad_kernel,
        grid=(pl.cdiv(units, tile),),
        in_specs=[
            pl.BlockSpec((None, tile, width), lambda i: (k, i, 0)),
            pl.BlockSpec((rows, width), lambda i: (0, 0)),
        ],
        out_specs=pl.BlockSpec((tile, rows), lambda i: (i, 0)),
        out_shape=jax.ShapeDtypeStruct((units, rows), BF16),
        cost_estimate=pl.CostEstimate(flops=1024, bytes_accessed=1024, transcendentals=0),
        compiler_params=pltpu.CompilerParams(vmem_limit_bytes=12 * 1024 * 1024),
        name="hidden_grad",
    )(weights, de)


def normed(embed):
    e32 = embed.astype(F32)
    inverse = lax.rsqrt(jnp.sum(e32 * e32, axis=-1, keepdims=True) + EPS)
    return (e32 * inverse, inverse)


def embed_grad(z32, inverse, dz):
    return ((dz - z32 * jnp.sum(z32 * dz, axis=-1, keepdims=True)) * inverse).astype(BF16)


def body(
    img_embed,
    txt_embed,
    img_hidden,
    txt_hidden,
    proj_weights,
    residual_in,
    partner,
    group_ids,
    logit_scale,
    logit_bias,
    loss_scale,
):
    here = lax.axis_index("blk")
    tp = lax.axis_index("tp")
    x_hi, z, core = here // 8, (here // 2) % 4, here % 2
    half = tp ^ x_hi
    rows, width = img_embed.shape[1:]
    share, quarter = rows // 2, rows // 4
    pod = rows * lax.axis_size("blk")
    scale = logit_scale[0]
    bias = logit_bias[0]
    factor = loss_scale[0] / pod
    line = Line()

    ids = partner[0]
    other_ids = swap_tp(ids)
    zt32, inv_t = normed(lax.dynamic_slice_in_dim(txt_embed[0], half * share, share, 0))
    texts = zt32.astype(BF16)
    line.mark(texts)
    low, high = texts[:quarter], texts[quarter:]
    low_cross = send_cross(low, 1, 0)
    high_ring = [send_cross(high, 0, dz) for dz in RING]

    img, other_ids = line.ready(img_embed[0], other_ids)
    ids = jnp.where(tp == 0, jnp.concatenate([ids, other_ids]), jnp.concatenate([other_ids, ids]))
    zi32, inv_i = normed(img)
    digits = jnp.stack([ids // DIGIT, ids % DIGIT]).astype(BF16)
    digits = jnp.pad(digits, ((0, 14), (0, width - rows)))
    own_images = jnp.concatenate([zi32.astype(BF16), digits])
    line.mark(own_images)
    core_images = swap_core(own_images)

    low_pair = jnp.concatenate(line.ready(low, low_cross))
    line.mark(low_pair)
    low_ring = [send_cross(low_pair, 0, dz) for dz in RING]
    high_all = jnp.concatenate(line.ready(high, *high_ring))
    line.mark(high_all)
    high_cross = send_cross(high_all, 1, 0)
    core_images = line.ready(core_images)
    images = jnp.concatenate([own_images[:rows], core_images[:rows]])
    digits = core_images[rows : rows + 2, :rows].astype(jnp.int32)
    ids = jnp.concatenate([ids, digits[0] * DIGIT + digits[1]])
    offsets = jnp.arange(quarter, dtype=jnp.int32)

    def column_ids(place):
        across, dz, start = place
        chip = (x_hi ^ across) * 4 + (z ^ dz)
        return (chip * 2 + core) * rows + half * share + start + offsets

    def products(block, places):
        columns = jnp.concatenate([column_ids(place) for place in places])
        logits = (
            scale * jnp.einsum("ie,je->ij", images, block, preferred_element_type=F32) + bias
        )
        positive = (ids[:, None] == columns[None, :]).astype(F32)
        weights = ((jax.nn.sigmoid(logits) - positive) * factor).astype(BF16)
        to_txt = jnp.einsum("ij,ie->je", weights, images, preferred_element_type=F32)
        return to_txt, weights

    def to_images(weights, block):
        return jnp.einsum("ij,je->ie", weights, block, preferred_element_type=F32)

    block = jnp.concatenate([low_pair, high_all])
    near_txt, weights = products(
        block, [(0, 0, 0), (1, 0, 0), (0, 0, quarter)] + [(0, dz, quarter) for dz in RING]
    )
    near_img = to_images(weights, block)
    line.mark(near_txt, near_img)
    block = jnp.concatenate(line.ready(*low_ring, high_cross))
    far_txt, weights = products(
        block,
        [(across, dz, 0) for dz in RING for across in (0, 1)]
        + [(1, dz, quarter) for dz in (0,) + RING],
    )
    far_send = far_txt.astype(BF16)
    line.mark(far_send)
    high_back = send_cross(far_send[3 * share :], 1, 0)
    low_back = [
        send_cross(far_send[i * share : (i + 1) * share], 0, dz) for i, dz in enumerate(RING)
    ]

    img_grad = near_img + to_images(line.ready(weights), block)
    img_core = img_grad[rows:].astype(BF16)
    line.mark(img_core)
    img_grad = img_grad[:rows] + line.ready(swap_core(img_core)).astype(F32)
    img_send = img_grad.astype(BF16)
    line.mark(img_send)
    img_other = swap_tp(img_send)

    img_other, high_back, *low_back = line.ready(img_other, high_back, *low_back)

    def low_part(i, near_txt, low_back):
        total = near_txt[i * quarter : (i + 1) * quarter]
        for part in low_back:
            total = total + part[i * quarter : (i + 1) * quarter].astype(F32)
        return total

    def high_part(i, near_txt, high_back):
        here = slice(i * quarter, (i + 1) * quarter)
        return near_txt[share:][here] + high_back[here].astype(F32)

    low_send = low_part(1, near_txt, low_back).astype(BF16)
    high_send = [high_part(i, near_txt, high_back).astype(BF16) for i in (1, 2, 3)]
    line.mark(low_send, *high_send)
    low_last = send_cross(low_send, 1, 0)
    high_last = [send_cross(value, 0, dz) for value, dz in zip(high_send, RING)]

    units = img_hidden.shape[2]
    tiles = (2, 4, width // 16, units)

    def pick(value, i):
        return lax.dynamic_index_in_dim(value, i, 0, keepdims=False)

    def both(split, x_from, z_from, x_count, z_count):
        sizes = (x_count, z_count, width // 16, units)
        places = (x_from, z_from, 0, 0)
        mine, got = split
        return lax.dynamic_slice(mine, places, sizes).astype(F32) + lax.dynamic_slice(
            got, places, sizes
        ).astype(F32)

    near_txt, high_back, low_last, *parts = line.ready(
        near_txt, high_back, low_last, *low_back, *high_last
    )
    low_sum = low_part(0, near_txt, parts[:3]) + low_last.astype(F32)
    high_sum = high_part(0, near_txt, high_back)
    for part in parts[3:]:
        high_sum = high_sum + part.astype(F32)
    de_half = embed_grad(zt32, inv_t, scale * jnp.concatenate([low_sum, high_sum]))
    line.mark(de_half)
    de_other = swap_tp(de_half)

    img_grad = img_grad + line.ready(img_other).astype(F32)
    de_img = embed_grad(zi32, inv_i, scale * img_grad)
    line.mark(de_img)
    de_half, de_other = line.ready(de_half, de_other)
    de_txt = jnp.where(
        half == 0, jnp.concatenate([de_half, de_other]), jnp.concatenate([de_other, de_half])
    )
    txt_mine, txt_other = split_grad(core, de_txt, txt_hidden[0])
    line.mark(txt_other)
    txt_got = swap_core(txt_other)
    img_mine, img_other = split_grad(core, line.ready(de_img), img_hidden[0])
    line.mark(img_other)
    img_got = swap_core(img_other)

    txt_split = (txt_mine.reshape(tiles), line.ready(txt_got).reshape(tiles))
    leave = [both(txt_split, 0, z ^ dz, 2, 1).astype(BF16) for dz in RING]
    line.mark(*leave)
    txt_parts = [send_far(value, 0, dz) for value, dz in zip(leave, RING)]
    img_split = (img_mine.reshape(tiles), line.ready(img_got).reshape(tiles))
    leave = both(img_split, 1 - x_hi, 0, 1, 4).astype(BF16)
    line.mark(leave)
    img_cross = send_far(leave, 1, 0)
    d_txt = hidden_grad(proj_weights, 1, line.ready(de_txt))
    line.mark(d_txt)
    d_img = hidden_grad(proj_weights, 0, line.ready(de_img))
    line.mark(d_img)

    def chunk(split, x_from, z_from):
        return both(split, x_from, z_from, 1, 1)[0, 0]

    def txt_chunk(parts, x_from):
        total = chunk(txt_split, x_from, z)
        for part in parts:
            total = total + pick(part[:, 0], x_from).astype(F32)
        return total

    def img_chunk(part, z_from):
        return chunk(img_split, x_hi, z_from) + pick(part[0], z_from).astype(F32)

    txt_parts = line.ready(*txt_parts)
    leave = txt_chunk(txt_parts, 1 - x_hi).astype(BF16)
    line.mark(leave)
    txt_cross = send_far(leave, 1, 0)
    grad_txt = txt_chunk(line.ready(*txt_parts), x_hi)
    line.mark(grad_txt)
    img_cross = line.ready(img_cross)
    leave = [img_chunk(img_cross, z ^ dz).astype(BF16) for dz in RING]
    line.mark(*leave)
    img_parts = [send_far(value, 0, dz) for value, dz in zip(leave, RING)]

    onehots = [
        (group_ids[k][None, :] == jnp.arange(NG, dtype=jnp.int32)[:, None]).astype(F32)
        for k in range(2)
    ]
    counts = [jnp.sum(onehot, axis=1) * residual_in.shape[1] for onehot in onehots]

    def packed_of(g_total, k):
        absum = jnp.sum(jnp.abs(g_total), axis=0)
        group_total = jnp.sum(onehots[k] * absum[None, :], axis=1)
        level = group_total / counts[k] + EPS
        spread = jnp.sum(onehots[k] * level[:, None], axis=0)[None]
        return spread * jnp.tanh(g_total / spread)

    def pods(packed):
        return [packed, send_pod(packed, 2), send_pod(packed, 1), send_pod(packed, 3)]

    def pod_sum(parts):
        own, far, up, down = (part.astype(F32) for part in parts)
        return (own + far) + (up + down)

    g_txt = grad_txt + line.ready(txt_cross).astype(F32) + residual_in[0, :, 1]
    packed_txt = packed_of(g_txt, 1)
    txt_pods = pods(packed_txt.astype(BF16))
    line.mark(txt_pods[0])
    grad_img = img_chunk(line.ready(img_cross), z)
    line.mark(grad_img)
    for part in line.ready(*img_parts):
        grad_img = grad_img + part.astype(F32)
    g_img = grad_img + residual_in[0, :, 0]
    packed_img = packed_of(g_img, 0)
    img_pods = pods(packed_img.astype(BF16))
    line.mark(img_pods[0])
    sum_txt = pod_sum(line.ready(*txt_pods))
    line.mark(sum_txt)
    residual = jnp.stack([g_img - packed_img, g_txt - packed_txt], 1)
    summed = jnp.stack([pod_sum(line.ready(*img_pods)), sum_txt], 1)
    return (d_img.T[None], d_txt.T[None], summed, residual[None])


def solution(mesh):
    placed = (
        P("outer", "blk", None),
        P("outer", "blk", None),
        P("outer", "blk", "tp"),
        P("outer", "blk", "tp"),
        P(None, "tp", None),
        P("outer", "blk", None, "tp"),
        P("outer", ("blk", "tp")),
        P(None, "tp"),
        P(),
        P(),
        P(),
    )
    return jax.shard_map(
        body,
        mesh=mesh,
        in_specs=placed,
        out_specs=(
            P("outer", "blk", "tp"),
            P("outer", "blk", "tp"),
            P("blk", None, "tp"),
            P("outer", "blk", None, "tp"),
        ),
        check_vma=False,
    )
```

```python
import jax
import jax.numpy as jnp
from jax import lax
from jax.experimental import pallas as pl
from jax.experimental.pallas import tpu as pltpu
from jax.sharding import PartitionSpec as P

NG = 8
EPS = 1e-06
AXES = ("outer", "blk", "tp")
F32 = jnp.float32
BF16 = jnp.bfloat16


def moved(where):
    pairs = []
    for y in range(4):
        for x in range(4):
            for z in range(4):
                for c in range(2):
                    x2, y2, z2, c2 = where(x, y, z, c)
                    place = lambda x, y, z, c: (y * 16 + (x // 2) * 8 + z * 2 + c) * 2 + x % 2
                    pairs.append((place(x, y, z, c), place(x2 % 4, y2 % 4, z2 % 4, c2)))
    return pairs


def send(value, where):
    return lax.ppermute(value, AXES, moved(where))


def swap_core(value):
    return send(value, lambda x, y, z, c: (x, y, z, 1 - c))


def swap_tp(value):
    return send(value, lambda x, y, z, c: (x ^ 1, y, z, c))


def send_cross(value, across, dz):
    return send(value, lambda x, y, z, c: (3 - x if across else x, y, z ^ dz, c))


def send_far(value, across, dz):
    return send(value, lambda x, y, z, c: (x + 2 * across, y, z ^ dz, c))


def send_pod(value, dy):
    return send(value, lambda x, y, z, c: (x, y ^ dy, z, c))


RING = (1, 3, 2)
DIGIT = 64


class Line:
    def __init__(self):
        self.marked = ()

    def ready(self, *values):
        values = lax.optimization_barrier((*values, *self.marked))[: len(values)]
        return values[0] if len(values) == 1 else values

    def mark(self, *values):
        self.marked = values


def split_grad_kernel(core, de, hidden, mine, other, turned):
    half = turned.shape[0] // 2

    @pl.when(pl.program_id(0) == 0)
    def _():
        flat = de[...].astype(F32).T
        rows = flat.shape[0] // 16
        pieces = [flat[i * rows : (i + 1) * rows] for i in range(16)]
        even, odd = jnp.concatenate(pieces[0::2]), jnp.concatenate(pieces[1::2])
        first = core[0] == 0
        turned[:half] = jnp.where(first, even, odd).astype(BF16)
        turned[half:] = jnp.where(first, odd, even).astype(BF16)

    for out, rows in ((mine, slice(0, half)), (other, slice(half, None))):
        out[...] = lax.dot_general(
            turned[rows], hidden[...], (((1,), (1,)), ((), ())), preferred_element_type=F32
        ).astype(BF16)


def split_grad(core, de, hidden):
    rows, width = de.shape
    units = hidden.shape[1]
    tile = 1152
    block = pl.BlockSpec((width // 2, tile), lambda i: (0, i))
    return pl.pallas_call(
        split_grad_kernel,
        grid=(pl.cdiv(units, tile),),
        in_specs=[
            pl.BlockSpec(memory_space=pltpu.SMEM),
            pl.BlockSpec((rows, width), lambda i: (0, 0)),
            pl.BlockSpec((tile, rows), lambda i: (i, 0)),
        ],
        out_specs=[block, block],
        out_shape=[pltpu.HBM((width // 2, units), BF16)] * 2,
        scratch_shapes=[pltpu.VMEM((width, rows), BF16)],
        cost_estimate=pl.CostEstimate(flops=1024, bytes_accessed=1024, transcendentals=0),
        compiler_params=pltpu.CompilerParams(vmem_limit_bytes=16 * 1024 * 1024),
        name="split_grad",
    )(jnp.reshape(core, (1,)), de, hidden.T)


def hidden_grad_kernel(weights, de, out):
    out[...] = lax.dot_general(
        weights[...], de[...], (((1,), (1,)), ((), ())), preferred_element_type=F32
    ).astype(BF16)


def hidden_grad(weights, k, de):
    rows, width = de.shape
    units = weights.shape[1]
    tile = 1088
    return pl.pallas_call(
        hidden_grad_kernel,
        grid=(pl.cdiv(units, tile),),
        in_specs=[
            pl.BlockSpec((None, tile, width), lambda i: (k, i, 0)),
            pl.BlockSpec((rows, width), lambda i: (0, 0)),
        ],
        out_specs=pl.BlockSpec((tile, rows), lambda i: (i, 0)),
        out_shape=jax.ShapeDtypeStruct((units, rows), BF16),
        cost_estimate=pl.CostEstimate(flops=1024, bytes_accessed=1024, transcendentals=0),
        compiler_params=pltpu.CompilerParams(vmem_limit_bytes=12 * 1024 * 1024),
        name="hidden_grad",
    )(weights, de)


def normed_rows_kernel(first, embed, out, inverse):
    e32 = embed[pl.ds(pl.multiple_of(first[0], 128), 128), :].astype(F32)
    inv = lax.rsqrt(jnp.sum(e32 * e32, axis=-1, keepdims=True) + EPS)
    inverse[...] = inv
    out[...] = (e32 * inv).astype(BF16)


def normed_rows(embed, first):
    width = embed.shape[1]
    return pl.pallas_call(
        normed_rows_kernel,
        in_specs=[pl.BlockSpec(memory_space=pltpu.SMEM), pl.BlockSpec(memory_space=pltpu.VMEM)],
        out_specs=[pl.BlockSpec(memory_space=pltpu.VMEM)] * 2,
        out_shape=[
            jax.ShapeDtypeStruct((128, width), BF16),
            jax.ShapeDtypeStruct((128, 1), F32),
        ],
        cost_estimate=pl.CostEstimate(flops=1024, bytes_accessed=1024, transcendentals=0),
        compiler_params=pltpu.CompilerParams(vmem_limit_bytes=8 * 1024 * 1024),
        name="normed_rows",
    )(jnp.reshape(first, (1,)), embed)


def normed(embed):
    e32 = embed.astype(F32)
    inverse = lax.rsqrt(jnp.sum(e32 * e32, axis=-1, keepdims=True) + EPS)
    return (e32 * inverse, inverse)


def embed_grad(z32, inverse, dz):
    return ((dz - z32 * jnp.sum(z32 * dz, axis=-1, keepdims=True)) * inverse).astype(BF16)


def body(
    img_embed,
    txt_embed,
    img_hidden,
    txt_hidden,
    proj_weights,
    residual_in,
    partner,
    group_ids,
    logit_scale,
    logit_bias,
    loss_scale,
):
    here = lax.axis_index("blk")
    tp = lax.axis_index("tp")
    x_hi, z, core = here // 8, (here // 2) % 4, here % 2
    half = tp ^ x_hi
    rows, width = img_embed.shape[1:]
    share, quarter = rows // 2, rows // 4
    pod = rows * lax.axis_size("blk")
    scale = logit_scale[0]
    bias = logit_bias[0]
    factor = loss_scale[0] / pod
    line = Line()

    ids = partner[0]
    other_ids = swap_tp(ids)
    texts, inv_t = normed_rows(txt_embed[0], half * share)
    line.mark(texts)
    low, high = texts[:quarter], texts[quarter:]
    low_cross = send_cross(low, 1, 0)
    high_ring = [send_cross(high, 0, dz) for dz in RING]

    img, other_ids = line.ready(img_embed[0], other_ids)
    ids = jnp.where(tp == 0, jnp.concatenate([ids, other_ids]), jnp.concatenate([other_ids, ids]))
    zi32, inv_i = normed(img)
    digits = jnp.stack([ids // DIGIT, ids % DIGIT]).astype(BF16)
    digits = jnp.pad(digits, ((0, 14), (0, width - rows)))
    own_images = jnp.concatenate([zi32.astype(BF16), digits])
    line.mark(own_images)
    core_images = swap_core(own_images)

    low_pair = jnp.concatenate(line.ready(low, low_cross))
    line.mark(low_pair)
    low_ring = [send_cross(low_pair, 0, dz) for dz in RING]
    high_all = jnp.concatenate(line.ready(high, *high_ring))
    line.mark(high_all)
    high_cross = send_cross(high_all, 1, 0)
    core_images = line.ready(core_images)
    images = jnp.concatenate([own_images[:rows], core_images[:rows]])
    digits = core_images[rows : rows + 2, :rows].astype(jnp.int32)
    ids = jnp.concatenate([ids, digits[0] * DIGIT + digits[1]])
    offsets = jnp.arange(quarter, dtype=jnp.int32)

    def column_ids(place):
        across, dz, start = place
        chip = (x_hi ^ across) * 4 + (z ^ dz)
        return (chip * 2 + core) * rows + half * share + start + offsets

    def products(block, places):
        columns = jnp.concatenate([column_ids(place) for place in places])
        logits = (
            scale * jnp.einsum("ie,je->ij", images, block, preferred_element_type=F32) + bias
        )
        positive = (ids[:, None] == columns[None, :]).astype(F32)
        weights = ((jax.nn.sigmoid(logits) - positive) * factor).astype(BF16)
        to_txt = jnp.einsum("ij,ie->je", weights, images, preferred_element_type=F32)
        return to_txt, weights

    def to_images(weights, block):
        return jnp.einsum("ij,je->ie", weights, block, preferred_element_type=F32)

    block = jnp.concatenate([low_pair, high_all])
    near_txt, weights = products(
        block, [(0, 0, 0), (1, 0, 0), (0, 0, quarter)] + [(0, dz, quarter) for dz in RING]
    )
    near_img = to_images(weights, block)
    line.mark(near_txt, near_img)
    block = jnp.concatenate(line.ready(*low_ring, high_cross))
    far_txt, weights = products(
        block,
        [(across, dz, 0) for dz in RING for across in (0, 1)]
        + [(1, dz, quarter) for dz in (0,) + RING],
    )
    far_send = far_txt.astype(BF16)
    line.mark(far_send)
    high_back = send_cross(far_send[3 * share :], 1, 0)
    low_back = [
        send_cross(far_send[i * share : (i + 1) * share], 0, dz) for i, dz in enumerate(RING)
    ]

    img_grad = near_img + to_images(line.ready(weights), block)
    img_core = img_grad[rows:].astype(BF16)
    line.mark(img_core)
    img_grad = img_grad[:rows] + line.ready(swap_core(img_core)).astype(F32)
    img_send = img_grad.astype(BF16)
    line.mark(img_send)
    img_other = swap_tp(img_send)

    img_other, high_back, *low_back = line.ready(img_other, high_back, *low_back)

    def low_part(i, near_txt, low_back):
        total = near_txt[i * quarter : (i + 1) * quarter]
        for part in low_back:
            total = total + part[i * quarter : (i + 1) * quarter].astype(F32)
        return total

    def high_part(i, near_txt, high_back):
        here = slice(i * quarter, (i + 1) * quarter)
        return near_txt[share:][here] + high_back[here].astype(F32)

    low_send = low_part(1, near_txt, low_back).astype(BF16)
    high_send = [high_part(i, near_txt, high_back).astype(BF16) for i in (1, 2, 3)]
    line.mark(low_send, *high_send)
    low_last = send_cross(low_send, 1, 0)
    high_last = [send_cross(value, 0, dz) for value, dz in zip(high_send, RING)]

    units = img_hidden.shape[2]
    tiles = (2, 4, width // 16, units)

    def pick(value, i):
        return lax.dynamic_index_in_dim(value, i, 0, keepdims=False)

    def both(split, x_from, z_from, x_count, z_count):
        sizes = (x_count, z_count, width // 16, units)
        places = (x_from, z_from, 0, 0)
        mine, got = split
        return lax.dynamic_slice(mine, places, sizes).astype(F32) + lax.dynamic_slice(
            got, places, sizes
        ).astype(F32)

    near_txt, high_back, low_last, *parts = line.ready(
        near_txt, high_back, low_last, *low_back, *high_last
    )
    low_sum = low_part(0, near_txt, parts[:3]) + low_last.astype(F32)
    high_sum = high_part(0, near_txt, high_back)
    for part in parts[3:]:
        high_sum = high_sum + part.astype(F32)
    own_rows = lax.dynamic_slice_in_dim(txt_embed[0], half * share, share, 0)
    zt32 = own_rows.astype(F32) * inv_t
    de_half = embed_grad(zt32, inv_t, scale * jnp.concatenate([low_sum, high_sum]))
    line.mark(de_half)
    de_other = swap_tp(de_half)

    img_grad = img_grad + line.ready(img_other).astype(F32)
    de_img = embed_grad(zi32, inv_i, scale * img_grad)
    line.mark(de_img)
    de_half, de_other = line.ready(de_half, de_other)
    de_txt = jnp.where(
        half == 0, jnp.concatenate([de_half, de_other]), jnp.concatenate([de_other, de_half])
    )
    txt_mine, txt_other = split_grad(core, de_txt, txt_hidden[0])
    line.mark(txt_other)
    txt_got = swap_core(txt_other)
    img_mine, img_other = split_grad(core, line.ready(de_img), img_hidden[0])
    line.mark(img_other)
    img_got = swap_core(img_other)

    txt_split = (txt_mine.reshape(tiles), line.ready(txt_got).reshape(tiles))
    leave = [both(txt_split, 0, z ^ dz, 2, 1).astype(BF16) for dz in RING]
    line.mark(*leave)
    txt_parts = [send_far(value, 0, dz) for value, dz in zip(leave, RING)]
    img_split = (img_mine.reshape(tiles), line.ready(img_got).reshape(tiles))
    leave = both(img_split, 1 - x_hi, 0, 1, 4).astype(BF16)
    line.mark(leave)
    img_cross = send_far(leave, 1, 0)
    d_txt = hidden_grad(proj_weights, 1, line.ready(de_txt))
    line.mark(d_txt)
    d_img = hidden_grad(proj_weights, 0, line.ready(de_img))
    line.mark(d_img)

    def chunk(split, x_from, z_from):
        return both(split, x_from, z_from, 1, 1)[0, 0]

    def txt_chunk(parts, x_from):
        total = chunk(txt_split, x_from, z)
        for part in parts:
            total = total + pick(part[:, 0], x_from).astype(F32)
        return total

    def img_chunk(part, z_from):
        return chunk(img_split, x_hi, z_from) + pick(part[0], z_from).astype(F32)

    txt_parts = line.ready(*txt_parts)
    leave = txt_chunk(txt_parts, 1 - x_hi).astype(BF16)
    line.mark(leave)
    txt_cross = send_far(leave, 1, 0)
    grad_txt = txt_chunk(line.ready(*txt_parts), x_hi)
    line.mark(grad_txt)
    img_cross = line.ready(img_cross)
    leave = [img_chunk(img_cross, z ^ dz).astype(BF16) for dz in RING]
    line.mark(*leave)
    img_parts = [send_far(value, 0, dz) for value, dz in zip(leave, RING)]

    onehots = [
        (group_ids[k][None, :] == jnp.arange(NG, dtype=jnp.int32)[:, None]).astype(F32)
        for k in range(2)
    ]
    counts = [jnp.sum(onehot, axis=1) * residual_in.shape[1] for onehot in onehots]

    def packed_of(g_total, k):
        absum = jnp.sum(jnp.abs(g_total), axis=0)
        group_total = jnp.sum(onehots[k] * absum[None, :], axis=1)
        level = group_total / counts[k] + EPS
        spread = jnp.sum(onehots[k] * level[:, None], axis=0)[None]
        return spread * jnp.tanh(g_total / spread)

    middle = units // 256 * 128

    def one_swap(packed):
        packed = packed.astype(BF16)
        own = (packed[:, :middle], packed[:, middle:])
        line.mark(*own)
        return own, (send_pod(own[0], 1), send_pod(own[1], 3))

    def other_swap(own, got):
        own = [
            (a.astype(F32) + b.astype(F32)).astype(BF16) for a, b in zip(own, line.ready(*got))
        ]
        line.mark(*own)
        return own, (send_pod(own[0], 3), send_pod(own[1], 1))

    def pod_sum(own, got):
        return jnp.concatenate([a.astype(F32) + b.astype(F32) for a, b in zip(own, got)], axis=1)

    grad_img = img_chunk(line.ready(img_cross), z)
    line.mark(grad_img)
    g_txt = grad_txt + line.ready(txt_cross).astype(F32) + residual_in[0, :, 1]
    packed_txt = packed_of(g_txt, 1)
    txt_pods = one_swap(packed_txt)
    for part in line.ready(*img_parts):
        grad_img = grad_img + part.astype(F32)
    g_img = grad_img + residual_in[0, :, 0]
    packed_img = packed_of(g_img, 0)
    img_pods = one_swap(packed_img)
    txt_pods = other_swap(*txt_pods)
    img_pods = other_swap(*img_pods)
    sum_txt = pod_sum(txt_pods[0], line.ready(*txt_pods[1]))
    line.mark(sum_txt)
    residual = jnp.stack([g_img - packed_img, g_txt - packed_txt], 1)
    summed = jnp.stack([pod_sum(img_pods[0], line.ready(*img_pods[1])), sum_txt], 1)
    return (d_img.T[None], d_txt.T[None], summed, residual[None])


def solution(mesh):
    placed = (
        P("outer", "blk", None),
        P("outer", "blk", None),
        P("outer", "blk", "tp"),
        P("outer", "blk", "tp"),
        P(None, "tp", None),
        P("outer", "blk", None, "tp"),
        P("outer", ("blk", "tp")),
        P(None, "tp"),
        P(),
        P(),
        P(),
    )
    return jax.shard_map(
        body,
        mesh=mesh,
        in_specs=placed,
        out_specs=(
            P("outer", "blk", "tp"),
            P("outer", "blk", "tp"),
            P("blk", None, "tp"),
            P("outer", "blk", None, "tp"),
        ),
        check_vma=False,
    )
```

```python
import jax
import jax.numpy as jnp
from jax import lax
from jax.experimental import pallas as pl
from jax.experimental.pallas import tpu as pltpu
from jax.sharding import PartitionSpec as P

NG = 8
EPS = 1e-06
AXES = ("outer", "blk", "tp")
F32 = jnp.float32
BF16 = jnp.bfloat16


def moved(where):
    pairs = []
    for y in range(4):
        for x in range(4):
            for z in range(4):
                for c in range(2):
                    x2, y2, z2, c2 = where(x, y, z, c)
                    place = lambda x, y, z, c: (y * 16 + (x // 2) * 8 + z * 2 + c) * 2 + x % 2
                    pairs.append((place(x, y, z, c), place(x2 % 4, y2 % 4, z2 % 4, c2)))
    return pairs


def send(value, where):
    return lax.ppermute(value, AXES, moved(where))


def swap_core(value):
    return send(value, lambda x, y, z, c: (x, y, z, 1 - c))


def swap_tp(value):
    return send(value, lambda x, y, z, c: (x ^ 1, y, z, c))


def send_cross(value, across, dz):
    return send(value, lambda x, y, z, c: (3 - x if across else x, y, z ^ dz, c))


def send_far(value, across, dz):
    return send(value, lambda x, y, z, c: (x + 2 * across, y, z ^ dz, c))


def send_pod(value, dy):
    return send(value, lambda x, y, z, c: (x, y ^ dy, z, c))


RING = (1, 3, 2)
DIGIT = 64


class Line:
    def __init__(self):
        self.marked = ()

    def ready(self, *values):
        values = lax.optimization_barrier((*values, *self.marked))[: len(values)]
        return values[0] if len(values) == 1 else values

    def mark(self, *values):
        self.marked = values


def split_grad_kernel(core, de, hidden, mine, other, turned):
    half = turned.shape[0] // 2

    @pl.when(pl.program_id(0) == 0)
    def _():
        flat = de[...].astype(F32).T
        rows = flat.shape[0] // 16
        pieces = [flat[i * rows : (i + 1) * rows] for i in range(16)]
        even, odd = jnp.concatenate(pieces[0::2]), jnp.concatenate(pieces[1::2])
        first = core[0] == 0
        turned[:half] = jnp.where(first, even, odd).astype(BF16)
        turned[half:] = jnp.where(first, odd, even).astype(BF16)

    for out, rows in ((mine, slice(0, half)), (other, slice(half, None))):
        out[...] = lax.dot_general(
            turned[rows], hidden[...], (((1,), (1,)), ((), ())), preferred_element_type=F32
        ).astype(BF16)


def split_grad(core, de, hidden):
    rows, width = de.shape
    units = hidden.shape[1]
    tile = 1152
    block = pl.BlockSpec((width // 2, tile), lambda i: (0, i))
    return pl.pallas_call(
        split_grad_kernel,
        grid=(pl.cdiv(units, tile),),
        in_specs=[
            pl.BlockSpec(memory_space=pltpu.SMEM),
            pl.BlockSpec((rows, width), lambda i: (0, 0)),
            pl.BlockSpec((tile, rows), lambda i: (i, 0)),
        ],
        out_specs=[block, block],
        out_shape=[pltpu.HBM((width // 2, units), BF16)] * 2,
        scratch_shapes=[pltpu.VMEM((width, rows), BF16)],
        cost_estimate=pl.CostEstimate(flops=1024, bytes_accessed=1024, transcendentals=0),
        compiler_params=pltpu.CompilerParams(vmem_limit_bytes=16 * 1024 * 1024),
        name="split_grad",
    )(jnp.reshape(core, (1,)), de, hidden.T)


def hidden_grad_kernel(weights, de, out):
    out[...] = lax.dot_general(
        weights[...], de[...], (((1,), (1,)), ((), ())), preferred_element_type=F32
    ).astype(BF16)


def hidden_grad(weights, k, de):
    rows, width = de.shape
    units = weights.shape[1]
    tile = 1088
    return pl.pallas_call(
        hidden_grad_kernel,
        grid=(pl.cdiv(units, tile),),
        in_specs=[
            pl.BlockSpec((None, tile, width), lambda i: (k, i, 0)),
            pl.BlockSpec((rows, width), lambda i: (0, 0)),
        ],
        out_specs=pl.BlockSpec((tile, rows), lambda i: (i, 0)),
        out_shape=jax.ShapeDtypeStruct((units, rows), BF16),
        cost_estimate=pl.CostEstimate(flops=1024, bytes_accessed=1024, transcendentals=0),
        compiler_params=pltpu.CompilerParams(vmem_limit_bytes=12 * 1024 * 1024),
        name="hidden_grad",
    )(weights, de)


def normed_rows_kernel(first, embed, out, inverse):
    e32 = embed[pl.ds(pl.multiple_of(first[0], 128), 128), :].astype(F32)
    inv = lax.rsqrt(jnp.sum(e32 * e32, axis=-1, keepdims=True) + EPS)
    inverse[...] = inv
    out[...] = (e32 * inv).astype(BF16)


def normed_rows(embed, first):
    width = embed.shape[1]
    return pl.pallas_call(
        normed_rows_kernel,
        in_specs=[pl.BlockSpec(memory_space=pltpu.SMEM), pl.BlockSpec(memory_space=pltpu.VMEM)],
        out_specs=[pl.BlockSpec(memory_space=pltpu.VMEM)] * 2,
        out_shape=[
            jax.ShapeDtypeStruct((128, width), BF16),
            jax.ShapeDtypeStruct((128, 1), F32),
        ],
        cost_estimate=pl.CostEstimate(flops=1024, bytes_accessed=1024, transcendentals=0),
        compiler_params=pltpu.CompilerParams(vmem_limit_bytes=8 * 1024 * 1024),
        name="normed_rows",
    )(jnp.reshape(first, (1,)), embed)


def normed(embed):
    e32 = embed.astype(F32)
    inverse = lax.rsqrt(jnp.sum(e32 * e32, axis=-1, keepdims=True) + EPS)
    return (e32 * inverse, inverse)


def embed_grad(z32, inverse, dz):
    return ((dz - z32 * jnp.sum(z32 * dz, axis=-1, keepdims=True)) * inverse).astype(BF16)


def body(
    img_embed,
    txt_embed,
    img_hidden,
    txt_hidden,
    proj_weights,
    residual_in,
    partner,
    group_ids,
    logit_scale,
    logit_bias,
    loss_scale,
):
    here = lax.axis_index("blk")
    tp = lax.axis_index("tp")
    x_hi, z, core = here // 8, (here // 2) % 4, here % 2
    half = tp ^ x_hi
    rows, width = img_embed.shape[1:]
    share, quarter = rows // 2, rows // 4
    pod = rows * lax.axis_size("blk")
    scale = logit_scale[0]
    bias = logit_bias[0]
    factor = loss_scale[0] / pod
    line = Line()

    ids = partner[0]
    other_ids = swap_tp(ids)
    texts, inv_t = normed_rows(txt_embed[0], half * share)
    line.mark(texts)
    low, high = texts[:quarter], texts[quarter:]
    low_cross = send_cross(low, 1, 0)
    high_ring = [send_cross(high, 0, dz) for dz in RING]

    img, other_ids = line.ready(img_embed[0], other_ids)
    ids = jnp.where(tp == 0, jnp.concatenate([ids, other_ids]), jnp.concatenate([other_ids, ids]))
    zi32, inv_i = normed(img)
    digits = jnp.stack([ids // DIGIT, ids % DIGIT]).astype(BF16)
    digits = jnp.pad(digits, ((0, 14), (0, width - rows)))
    own_images = jnp.concatenate([zi32.astype(BF16), digits])
    line.mark(own_images)
    core_images = swap_core(own_images)

    low_pair = jnp.concatenate(line.ready(low, low_cross))
    line.mark(low_pair)
    low_ring = [send_cross(low_pair, 0, dz) for dz in RING]
    high_all = jnp.concatenate(line.ready(high, *high_ring))
    line.mark(high_all)
    high_cross = send_cross(high_all, 1, 0)
    core_images = line.ready(core_images)
    images = jnp.concatenate([own_images[:rows], core_images[:rows]])
    digits = core_images[rows : rows + 2, :rows].astype(jnp.int32)
    ids = jnp.concatenate([ids, digits[0] * DIGIT + digits[1]])
    offsets = jnp.arange(quarter, dtype=jnp.int32)

    def column_ids(place):
        across, dz, start = place
        chip = (x_hi ^ across) * 4 + (z ^ dz)
        return (chip * 2 + core) * rows + half * share + start + offsets

    def products(block, places):
        columns = jnp.concatenate([column_ids(place) for place in places])
        logits = (
            scale * jnp.einsum("ie,je->ij", images, block, preferred_element_type=F32) + bias
        )
        positive = (ids[:, None] == columns[None, :]).astype(F32)
        weights = ((jax.nn.sigmoid(logits) - positive) * factor).astype(BF16)
        to_txt = jnp.einsum("ij,ie->je", weights, images, preferred_element_type=F32)
        return to_txt, weights

    def to_images(weights, block):
        return jnp.einsum("ij,je->ie", weights, block, preferred_element_type=F32)

    block = jnp.concatenate([low_pair, high_all])
    near_txt, weights = products(
        block, [(0, 0, 0), (1, 0, 0), (0, 0, quarter)] + [(0, dz, quarter) for dz in RING]
    )
    near_img = to_images(weights, block)
    line.mark(near_txt, near_img)
    block = jnp.concatenate(line.ready(*low_ring, high_cross))
    far_txt, weights = products(
        block,
        [(across, dz, 0) for dz in RING for across in (0, 1)]
        + [(1, dz, quarter) for dz in (0,) + RING],
    )
    far_send = far_txt.astype(BF16)
    line.mark(far_send)
    high_back = send_cross(far_send[3 * share :], 1, 0)
    low_back = [
        send_cross(far_send[i * share : (i + 1) * share], 0, dz) for i, dz in enumerate(RING)
    ]

    weights = line.ready(weights)
    img_core = (near_img[rows:] + to_images(weights[rows:], block)).astype(BF16)
    line.mark(img_core)
    img_core = swap_core(img_core)
    img_grad = near_img[:rows] + to_images(line.ready(weights)[:rows], block)
    img_grad = img_grad + line.ready(img_core).astype(F32)
    img_send = img_grad.astype(BF16)
    line.mark(img_send)
    img_other = swap_tp(img_send)

    img_other, high_back, *low_back = line.ready(img_other, high_back, *low_back)

    def low_part(i, near_txt, low_back):
        total = near_txt[i * quarter : (i + 1) * quarter]
        for part in low_back:
            total = total + part[i * quarter : (i + 1) * quarter].astype(F32)
        return total

    def high_part(i, near_txt, high_back):
        here = slice(i * quarter, (i + 1) * quarter)
        return near_txt[share:][here] + high_back[here].astype(F32)

    low_send = low_part(1, near_txt, low_back).astype(BF16)
    high_send = [high_part(i, near_txt, high_back).astype(BF16) for i in (1, 2, 3)]
    line.mark(low_send, *high_send)
    low_last = send_cross(low_send, 1, 0)
    high_last = [send_cross(value, 0, dz) for value, dz in zip(high_send, RING)]

    units = img_hidden.shape[2]
    tiles = (2, 4, width // 16, units)

    def pick(value, i):
        return lax.dynamic_index_in_dim(value, i, 0, keepdims=False)

    def both(split, x_from, z_from, x_count, z_count):
        sizes = (x_count, z_count, width // 16, units)
        places = (x_from, z_from, 0, 0)
        mine, got = split
        return lax.dynamic_slice(mine, places, sizes).astype(F32) + lax.dynamic_slice(
            got, places, sizes
        ).astype(F32)

    near_txt, high_back, low_last, *parts = line.ready(
        near_txt, high_back, low_last, *low_back, *high_last
    )
    low_sum = low_part(0, near_txt, parts[:3]) + low_last.astype(F32)
    high_sum = high_part(0, near_txt, high_back)
    for part in parts[3:]:
        high_sum = high_sum + part.astype(F32)
    own_rows = lax.dynamic_slice_in_dim(txt_embed[0], half * share, share, 0)
    zt32 = own_rows.astype(F32) * inv_t
    de_half = embed_grad(zt32, inv_t, scale * jnp.concatenate([low_sum, high_sum]))
    line.mark(de_half)
    de_other = swap_tp(de_half)

    img_grad = img_grad + line.ready(img_other).astype(F32)
    de_img = embed_grad(zi32, inv_i, scale * img_grad)
    line.mark(de_img)
    de_half, de_other = line.ready(de_half, de_other)
    de_txt = jnp.where(
        half == 0, jnp.concatenate([de_half, de_other]), jnp.concatenate([de_other, de_half])
    )
    txt_mine, txt_other = split_grad(core, de_txt, txt_hidden[0])
    line.mark(txt_other)
    txt_got = swap_core(txt_other)
    img_mine, img_other = split_grad(core, line.ready(de_img), img_hidden[0])
    line.mark(img_other)
    img_got = swap_core(img_other)

    txt_split = (txt_mine.reshape(tiles), line.ready(txt_got).reshape(tiles))
    leave = [both(txt_split, 0, z ^ dz, 2, 1).astype(BF16) for dz in RING]
    line.mark(*leave)
    txt_parts = [send_far(value, 0, dz) for value, dz in zip(leave, RING)]
    img_split = (img_mine.reshape(tiles), line.ready(img_got).reshape(tiles))
    leave = both(img_split, 1 - x_hi, 0, 1, 4).astype(BF16)
    line.mark(leave)
    img_cross = send_far(leave, 1, 0)
    d_txt = hidden_grad(proj_weights, 1, line.ready(de_txt))
    line.mark(d_txt)
    d_img = hidden_grad(proj_weights, 0, line.ready(de_img))
    line.mark(d_img)

    def chunk(split, x_from, z_from):
        return both(split, x_from, z_from, 1, 1)[0, 0]

    def txt_chunk(parts, x_from):
        total = chunk(txt_split, x_from, z)
        for part in parts:
            total = total + pick(part[:, 0], x_from).astype(F32)
        return total

    def img_chunk(part, z_from):
        return chunk(img_split, x_hi, z_from) + pick(part[0], z_from).astype(F32)

    txt_parts = line.ready(*txt_parts)
    leave = txt_chunk(txt_parts, 1 - x_hi).astype(BF16)
    line.mark(leave)
    txt_cross = send_far(leave, 1, 0)
    grad_txt = txt_chunk(line.ready(*txt_parts), x_hi)
    line.mark(grad_txt)
    img_cross = line.ready(img_cross)
    leave = [img_chunk(img_cross, z ^ dz).astype(BF16) for dz in RING]
    line.mark(*leave)
    img_parts = [send_far(value, 0, dz) for value, dz in zip(leave, RING)]

    onehots = [
        (group_ids[k][None, :] == jnp.arange(NG, dtype=jnp.int32)[:, None]).astype(F32)
        for k in range(2)
    ]
    counts = [jnp.sum(onehot, axis=1) * residual_in.shape[1] for onehot in onehots]

    def packed_of(g_total, k):
        absum = jnp.sum(jnp.abs(g_total), axis=0)
        group_total = jnp.sum(onehots[k] * absum[None, :], axis=1)
        level = group_total / counts[k] + EPS
        spread = jnp.sum(onehots[k] * level[:, None], axis=0)[None]
        return spread * jnp.tanh(g_total / spread)

    middle = units // 256 * 128

    def one_swap(packed):
        packed = packed.astype(BF16)
        own = (packed[:, :middle], packed[:, middle:])
        line.mark(*own)
        return own, (send_pod(own[0], 1), send_pod(own[1], 3))

    def other_swap(own, got):
        own = [
            (a.astype(F32) + b.astype(F32)).astype(BF16) for a, b in zip(own, line.ready(*got))
        ]
        line.mark(*own)
        return own, (send_pod(own[0], 3), send_pod(own[1], 1))

    def pod_sum(own, got):
        return jnp.concatenate([a.astype(F32) + b.astype(F32) for a, b in zip(own, got)], axis=1)

    grad_img = img_chunk(line.ready(img_cross), z)
    line.mark(grad_img)
    g_txt = grad_txt + line.ready(txt_cross).astype(F32) + residual_in[0, :, 1]
    packed_txt = packed_of(g_txt, 1)
    txt_pods = one_swap(packed_txt)
    for part in line.ready(*img_parts):
        grad_img = grad_img + part.astype(F32)
    g_img = grad_img + residual_in[0, :, 0]
    packed_img = packed_of(g_img, 0)
    img_pods = one_swap(packed_img)
    txt_pods = other_swap(*txt_pods)
    img_pods = other_swap(*img_pods)
    sum_txt = pod_sum(txt_pods[0], line.ready(*txt_pods[1]))
    line.mark(sum_txt)
    residual = jnp.stack([g_img - packed_img, g_txt - packed_txt], 1)
    summed = jnp.stack([pod_sum(img_pods[0], line.ready(*img_pods[1])), sum_txt], 1)
    return (d_img.T[None], d_txt.T[None], summed, residual[None])


def solution(mesh):
    placed = (
        P("outer", "blk", None),
        P("outer", "blk", None),
        P("outer", "blk", "tp"),
        P("outer", "blk", "tp"),
        P(None, "tp", None),
        P("outer", "blk", None, "tp"),
        P("outer", ("blk", "tp")),
        P(None, "tp"),
        P(),
        P(),
        P(),
    )
    return jax.shard_map(
        body,
        mesh=mesh,
        in_specs=placed,
        out_specs=(
            P("outer", "blk", "tp"),
            P("outer", "blk", "tp"),
            P("blk", None, "tp"),
            P("outer", "blk", None, "tp"),
        ),
        check_vma=False,
    )
```
